512 devices in a mesh: segment: 8 (over y, core), vocab: 64 (over z, x).
Axes of the slice: x: 4, y: 4, z: 16, core: 2. Of those that a mesh axis runs over, the one named last changes fastest.
Arguments:
- hidden: bfloat16 [16384, 8192], P('vocab', 'segment'), may hold values from -160 to 160
- norm_gain: float32 [8192], P('segment'), may hold values from 0.5 to 1.5
- head: bfloat16 [65536, 8192], P('vocab', 'segment'), may hold values from -3 to 3
- allowed: int32 [4, 16384], P(None, 'vocab'), may hold values from 0 to 127, as said below
- target_slot: int32 [16384], P('vocab'), may hold values from 0 to 3
- target_offset: int32 [16384], P('vocab'), may hold values from 0 to 511
Outputs:
- logprob: float32 [16384], P('vocab')
The draws below stay inside these ranges and needn't reach their ends.
Inputs may be any that keep to these rules, and one draw needn't show every extreme that they name: `allowed`: the 4 blocks of a token are distinct. Among the 256 tokens of one index of vocab, a block is named by at most 16 of them; in every draw some block is named by exactly 16 tokens of every index of vocab.
All inputs are finite; a program needn't handle non-finite values.
Results may differ from the reference program's by a relative error of at most 0.00083.
Values may be sent and summed in bfloat16 or wider, within the bound.
A program may use at most 64 MiB of HBM per device.

```python
import math
import jax
import jax.numpy as jnp
from jax import lax

D = 8192
BLOCK = 512
BLK_DEV = 2
A = 4
TOK_DEV = 256
TOKENS = 16384
V = 65536
CAPB = 16
N_VOCAB = 64


def head_row(key, index):
    row_key = jax.random.fold_in(jax.random.fold_in(key, 11), index)
    return jax.random.truncated_normal(row_key, -5.0, 5.0, (D,), jnp.float32) * (4.0 / math.sqrt(D))


def allowed_table(key):
    base_key = jax.random.fold_in(key, 23)
    blk_count = BLK_DEV * N_VOCAB
    hot_block = jax.random.randint(jax.random.fold_in(base_key, 1), (), 0, blk_count, dtype=jnp.int32)
    entry_ids = jnp.arange(A * TOK_DEV, dtype=jnp.int32)

    def one_source(source):
        source_key = jax.random.fold_in(base_key, source + 100)
        order = jax.random.permutation(jax.random.fold_in(source_key, 1), blk_count).astype(jnp.int32)
        hot_place = jnp.argmax(order == hot_block)
        order = order.at[hot_place].set(order[0]).at[0].set(hot_block)
        halves = jax.random.randint(jax.random.fold_in(source_key, 2), (blk_count // 2,), 0, CAPB + 1, dtype=jnp.int32)
        halves = halves.at[0].set(CAPB)
        run_sizes = jnp.stack([halves, CAPB - halves], axis=1).reshape(blk_count)
        run_ends = jnp.cumsum(run_sizes).astype(jnp.int32)
        run_index = jnp.sum((entry_ids[:, None] >= run_ends[None, :]).astype(jnp.int32), axis=1)
        return order[run_index].reshape(A, TOK_DEV)
    table = jax.vmap(one_source)(jnp.arange(N_VOCAB, dtype=jnp.int32))
    return table.transpose(1, 0, 2).reshape(A, TOKENS).astype(jnp.int32)


def draw_allowed(key, part):
    return allowed_table(key)


def draw_head(key, part):
    rows = jax.vmap(lambda index: head_row(key, index))(jnp.arange(V, dtype=jnp.int32))
    return rows.astype(jnp.bfloat16)


def draw_hidden(key, part):
    own_key = jax.random.fold_in(key, 37)
    column = jnp.arange(D, dtype=jnp.float32) / D
    values = jax.random.truncated_normal(own_key, -6.0, 6.0, (TOKENS, D), jnp.float32) * jnp.exp(column * math.log(3.0))[None, :]
    return values.astype(jnp.bfloat16)


def plant(drawn, key, least, high):
    longest = drawn.shape.index(max(drawn.shape))
    spots = []
    for shift in (0, 1):
        where = [jax.random.randint(jax.random.fold_in(key, axis), (), 0, length) for axis, length in enumerate(drawn.shape)]
        where[longest] = (where[longest] + shift) % drawn.shape[longest]
        spots.append(tuple(where))
    return drawn.at[spots[0]].set(least).at[spots[1]].set(high)


def setup_inputs(seed: int = 0) -> dict:
    arg_keys = jax.random.split(jax.random.key(seed), 7)
    return {
        "hidden": draw_hidden(jax.random.fold_in(arg_keys[6], 71), 0),
        "norm_gain": jnp.clip(1.0 + 0.1 * jax.random.normal(arg_keys[1], (D,), jnp.float32), 0.5, 1.5),
        "head": draw_head(jax.random.fold_in(arg_keys[6], 71), 0),
        "allowed": draw_allowed(jax.random.fold_in(arg_keys[6], 71), 0),
        "target_slot": plant(jax.random.randint(arg_keys[4], (TOKENS,), 0, A), jax.random.fold_in(arg_keys[4], 1), 0, A - 1).astype(jnp.int32),
        "target_offset": plant(jax.random.randint(arg_keys[5], (TOKENS,), 0, BLOCK), jax.random.fold_in(arg_keys[5], 1), 0, BLOCK - 1).astype(jnp.int32),
    }


def block_stats(logits, targets):
    peak_value = lax.optimization_barrier(jnp.max(logits, axis=-1))
    exp_total = lax.optimization_barrier(jnp.sum(jnp.exp(logits - peak_value[..., None]), axis=-1))
    column = lax.broadcasted_iota(jnp.int32, logits.shape, logits.ndim - 1)
    target_logit = lax.optimization_barrier(jnp.sum(jnp.where(column == targets[..., None], logits, jnp.zeros_like(logits)), axis=-1))
    return (peak_value, exp_total, target_logit)

def reference(hidden, norm_gain, head, allowed, target_slot, target_offset):
    widened = hidden.astype(jnp.float32)
    mean_square = lax.optimization_barrier(jnp.mean(widened * widened, axis=1))
    normed = (widened * lax.rsqrt(mean_square + 1e-05)[:, None] * norm_gain[None, :]).astype(jnp.bfloat16)
    blk_count = BLK_DEV * N_VOCAB
    grouped = allowed.reshape(A, N_VOCAB, TOK_DEV).transpose(1, 0, 2).reshape(N_VOCAB, A * TOK_DEV)
    onehot = (grouped[:, :, None] == jnp.arange(blk_count, dtype=jnp.int32)[None, None, :]).astype(jnp.int32)
    before = (jnp.cumsum(onehot, axis=1) - onehot).astype(jnp.int32)
    position = lax.optimization_barrier(jnp.sum(before * onehot, axis=2)).astype(jnp.int32)
    sources = jnp.arange(N_VOCAB, dtype=jnp.int32)[:, None]
    slot_index = ((grouped * N_VOCAB + sources) * CAPB + position).astype(jnp.int32)
    local_token = jnp.tile(jnp.arange(TOK_DEV, dtype=jnp.int32), A)[None, :]
    token_id = (sources * TOK_DEV + local_token).astype(jnp.int32)
    slot_total = blk_count * N_VOCAB * CAPB
    slot_token = jnp.full((slot_total,), TOKENS, jnp.int32).at[slot_index.reshape(-1)].set(token_id.reshape(-1))
    entry_choice = jnp.repeat(jnp.arange(A, dtype=jnp.int32), TOK_DEV)[None, :]
    slot_rep = jnp.tile(target_slot.reshape(N_VOCAB, TOK_DEV), (1, A))
    offset_rep = jnp.tile(target_offset.reshape(N_VOCAB, TOK_DEV), (1, A))
    entry_target = jnp.where(entry_choice == slot_rep, offset_rep, -1).astype(jnp.int32)
    slot_target = jnp.full((slot_total,), -1, jnp.int32).at[slot_index.reshape(-1)].set(entry_target.reshape(-1))
    padded = jnp.concatenate([normed, jnp.zeros((1, D), jnp.bfloat16)], axis=0)
    per_block = N_VOCAB * CAPB

    def one_block(block):
        begin = (block * per_block).astype(jnp.int32)
        ids = lax.dynamic_slice_in_dim(slot_token, begin, per_block, 0)
        rows = padded[ids]
        weights = lax.dynamic_slice_in_dim(head, (block * BLOCK).astype(jnp.int32), BLOCK, 0)
        logits = jnp.dot(rows, weights.T, preferred_element_type=jnp.float32)
        targets = lax.dynamic_slice_in_dim(slot_target, begin, per_block, 0)
        return block_stats(logits, targets)
    peak_value, exp_total, target_logit = lax.map(one_block, jnp.arange(blk_count, dtype=jnp.int32))
    flat_index = slot_index.reshape(-1)
    peak_value = peak_value.reshape(-1)[flat_index].reshape(N_VOCAB, A, TOK_DEV)
    exp_total = exp_total.reshape(-1)[flat_index].reshape(N_VOCAB, A, TOK_DEV)
    target_logit = target_logit.reshape(-1)[flat_index].reshape(N_VOCAB, A, TOK_DEV)
    largest = lax.optimization_barrier(jnp.max(peak_value, axis=1))
    log_total = largest + jnp.log(lax.optimization_barrier(jnp.sum(exp_total * jnp.exp(peak_value - largest[:, None, :]), axis=1)))
    return (lax.optimization_barrier(jnp.sum(target_logit, axis=1)) - log_total).reshape(TOKENS)
```

```python
import functools

import jax
import jax.numpy as jnp
from jax import lax
from jax.experimental import pallas as pl
from jax.experimental.pallas import tpu as pltpu
from jax.sharding import PartitionSpec as P

D = 8192
BLOCK = 512
A = 4
CAP = 16
NZ = 16
NX = 4
TOK = 256
SLAB = 1024
F32 = jnp.float32
BF16 = jnp.bfloat16
ROUND_A = ((0, 2, 0, 3),)
ROUND_B = ((0, 2, 3, 5), (2, 3, 0, 5))
ROUND_C = ((0, 3, 5, 6), (3, 4, 0, 6))
ROUND_D = ((0, 4, 6, 7),)
ROUND_E = ((0, 4, 7, 8),)
ROUNDS = ROUND_A + ROUND_B + ROUND_C + ROUND_D + ROUND_E


def kernel(
    hid,
    gain,
    head,
    allowed,
    tslot,
    toff,
    out,
    X,
    M,
    H,
    G,
    Pp,
    Pr,
    St,
    Rs,
    Rr,
    rcode,
    Sx,
    E,
    acc,
    xs,
    xr,
    ms,
    mr,
    hs,
    hr,
    ps,
    pr,
    ss,
    sr,
    es,
    er,
    ts,
    tr,
    own,
):
    seg = lax.axis_index("segment")
    v = lax.axis_index("vocab")
    z = v // NX
    x = lax.rem(v, NX)
    my_i = seg // 4
    my_h = lax.rem(seg // 2, 2)
    my_d = lax.rem(seg, 2)

    def at_z(step):
        return lax.rem(z + step + NZ, NZ) * NX + x

    def at_x(step):
        return z * NX + lax.rem(x + step + NX, NX)

    def push(src, dst, send, recv, s, d):
        return pltpu.make_async_remote_copy(
            src_ref=src,
            dst_ref=dst,
            send_sem=send,
            recv_sem=recv,
            device_id=(s, d),
            device_id_type=pl.DeviceIdType.MESH,
        )

    own_slab = pltpu.make_async_copy(hid, X.at[0, 7], own.at[0])
    own_slab.start()
    own_head = [
        pltpu.make_async_copy(head.at[pl.ds(i * BLOCK, BLOCK)], H.at[0, i], own.at[1 + i])
        for i in range(2)
    ]
    for c in own_head:
        c.start()

    barrier = pltpu.get_barrier_semaphore()
    for d in (at_z(1), at_z(-1), at_x(1), at_x(-1)):
        pl.semaphore_signal(
            barrier, inc=1, device_id=(seg, d), device_id_type=pl.DeviceIdType.MESH
        )
    for rel in range(1, 8):
        pl.semaphore_signal(
            barrier,
            inc=1,
            device_id=(lax.rem(seg + rel, 8), v),
            device_id_type=pl.DeviceIdType.MESH,
        )
    pl.semaphore_wait(barrier, 11)

    half = TOK // 2
    sides = (at_z(1), at_z(-1))

    def slab(k, d, c):
        rows = pl.ds(c * half, half)
        src = hid.at[rows] if k == 0 else X.at[d, k - 1, rows]
        dst = X.at[1, 7, rows] if k == 7 else X.at[d, k, rows]
        return push(src, dst, xs.at[d, k, c], xr.at[d, k, c], seg, sides[d])

    def meta(k, d):
        src = M.at[0, 7] if k == 0 else M.at[d, k - 1]
        dst = M.at[1, 7] if k == 7 else M.at[d, k]
        return push(src, dst, ms.at[d, k], mr.at[d, k], seg, sides[d])

    for c in range(2):
        for d in range(2):
            slab(0, d, c).start()

    first, second = head.at[pl.ds(0, BLOCK)], head.at[pl.ds(BLOCK, BLOCK)]

    def block(w, i):
        src = ((first, second), (second, first), (H.at[1, 0], H.at[1, 1]))[w - 1][i]
        return push(src, H.at[w, i], hs.at[w, i], hr.at[w, i], seg, at_x(1 - 2 * i))

    for i in range(2):
        block(1, i).start()

    tokens = lax.broadcasted_iota(jnp.int32, (TOK, TOK), 0)
    later = lax.broadcasted_iota(jnp.int32, (TOK, TOK), 1)
    upper = jnp.where(tokens < later, 1.0, 0.0).astype(BF16)
    blocks = lax.broadcasted_iota(jnp.int32, (128, TOK), 0)
    seen = jnp.zeros((128, 1), F32)
    codes = []
    for j in range(A):
        named = blocks == allowed[pl.ds(j, 1), :]
        hot = jnp.where(named, 1.0, 0.0)
        before = jnp.dot(hot.astype(BF16), upper, preferred_element_type=F32) + seen
        place = jnp.sum(jnp.where(named, before, 0.0), axis=0, keepdims=True)
        codes.append((allowed[pl.ds(j, 1), :] * CAP).astype(F32) + place)
        seen = seen + jnp.sum(hot, axis=1, keepdims=True)
    target = codes[0]
    for j in range(1, A):
        target = jnp.where(tslot[...] == j, codes[j], target)
    offset = toff[...].astype(F32)

    slot = lax.broadcasted_iota(jnp.int32, (CAP, TOK), 0)
    left, right, across = (lax.rem(x + s, NX) for s in (3, 1, 2))
    for i in range(2):
        for w in range(4):
            column = (x, (left, right)[i], (left, right)[i], across)[w]
            odd = (i, i, 1 - i, i)[w]
            which = (z * 8 + column * 2 + odd) * CAP
            rcode[i, pl.ds(w * CAP, CAP), :] = (slot + which).astype(F32)

    own_slab.wait()
    squares = jnp.zeros((TOK, 128), F32)
    for c in range(SLAB // 128):
        part = X[0, 7, :, pl.ds(c * 128, 128)].astype(F32)
        squares = squares + part * part
    Sx[0] = jnp.sum(squares.T.reshape(16, 8, TOK), axis=0)

    def square(rel):
        return push(
            Sx.at[0], Sx.at[rel], ss.at[rel], sr.at[rel], lax.rem(seg + rel, 8), v
        )

    for rel in range(1, 8):
        square(rel).start()
    total = Sx[0]
    for rel in range(1, 8):
        square(rel).wait_recv()
        total = total + Sx[rel]
    scale = lax.rsqrt(jnp.sum(total, axis=0, keepdims=True) * (1.0 / D) + 1e-05)
    M[0, 7] = jnp.concatenate(codes + [scale, target, offset, offset], axis=0)
    for d in range(2):
        meta(0, d).start()

    def gather(k, d):
        hit = None
        for i in range(2):
            info = M[d, k]
            rows = rcode[i]
            hit = rows == info[0:1, :]
            for j in range(1, A):
                hit = hit | (rows == info[j : j + 1, :])
            pick = jnp.where(hit, 1.0, 0.0).astype(BF16)
            picked = jnp.dot(pick, X[d, k], preferred_element_type=F32)
            size = jnp.sum(jnp.where(hit, info[4:5, :], 0.0), axis=1, keepdims=True)
            normed = (picked * size * gain[...]).astype(BF16)
            for w in range(4):
                G[w, i, k, d] = normed[w * CAP : (w + 1) * CAP]

    def products(w0, w1, k0, k1):
        count = k1 - k0

        def one(n, carry):
            w, i = n // 2, lax.rem(n, 2)
            rows = G[w, i, pl.ds(k0, count)].reshape(count * 2 * CAP, SLAB)
            logits = lax.dot_general(
                rows, H[w, i], (((1,), (1,)), ((), ())), preferred_element_type=F32
            )
            logits = logits.reshape(count, 2, CAP, BLOCK).astype(BF16)
            for d in range(2):
                for h in range(2):
                    Pp[4 * i + 2 * h + d, pl.ds(k0, count), w] = logits[
                        :, d, :, 256 * h : 256 * (h + 1)
                    ]
            return carry

        lax.fori_loop(2 * w0, 2 * w1, one, 0)

    def partial(r, rel):
        w0, w1, k0, k1 = ROUNDS[r]
        dest = lax.rem(seg + rel, 8)
        part = (pl.ds(k0, k1 - k0), pl.ds(w0, w1 - w0))
        return push(
            Pp.at[(dest, *part)],
            Pr.at[(rel, *part)],
            ps.at[r, rel],
            pr.at[r, rel],
            dest,
            v,
        )

    def send_round(rounds):
        for r in rounds:
            products(*ROUNDS[r])

            def one(rel, carry, r=r):
                partial(r, rel).start()
                return carry

            lax.fori_loop(1, 8, one, 0)

    def stats(rounds):
        for r in rounds:
            w0, w1, k0, k1 = ROUNDS[r]
            n = (w1 - w0) * CAP

            def arrive(rel, carry, r=r):
                partial(r, rel).wait_recv()
                return carry

            lax.fori_loop(1, 8, arrive, 0)

            def one(k, carry, w0=w0, w1=w1, n=n):
                span = pl.ds(w0, w1 - w0)
                logits = Pp[seg, k, span].reshape(n, 256).astype(F32)
                for rel in range(1, 8):
                    logits = logits + Pr[rel, k, span].reshape(n, 256).astype(F32)
                info = M[my_d, k]
                rows = rcode[my_i, pl.ds(w0 * CAP, n), :]
                wanted = jnp.sum(
                    jnp.where(rows == info[5:6, :], info[6:7, :] + 1.0, 0.0),
                    axis=1,
                    keepdims=True,
                )
                column = lax.broadcasted_iota(jnp.int32, (n, 256), 1) + 256 * my_h + 1
                peak = jnp.max(logits, axis=1, keepdims=True)
                mass = jnp.sum(jnp.exp(logits - peak), axis=1, keepdims=True)
                goal = jnp.sum(
                    jnp.where(column.astype(F32) == wanted, logits, 0.0),
                    axis=1,
                    keepdims=True,
                )
                lane = lax.broadcasted_iota(jnp.int32, (n, 128), 1)
                St[k, pl.ds(w0 * CAP, n), :] = jnp.where(
                    lane == 0, peak, jnp.where(lane == 1, mass, goal)
                )
                return carry

            lax.fori_loop(k0, k1, one, 0)

    def report(k):
        step = jnp.where(my_d == 0, -(k + 1), k + 1)
        return push(Rs.at[k], Rr.at[k], ts.at[k], tr.at[k], seg, at_z(step))

    def turn(k):
        rows = St[k]
        Rs[k] = jnp.concatenate([rows, rows], axis=0).T[0:8]

    acc[...] = jnp.zeros((16, TOK), F32)

    def collect(k, step):
        plane = lax.rem(z + step + NZ, NZ) - z
        rows = rcode[my_i] + (plane * 128).astype(F32)
        columns = jnp.concatenate([Rr[k]] * 16, axis=0).T
        for j in range(A):
            match = rows == M[0, 7, j : j + 1, :]
            for q in range(3):
                acc[pl.ds(4 * q + j, 1), :] += jnp.sum(
                    jnp.where(match, columns[0:64, q : q + 1], 0.0), axis=0, keepdims=True
                )

    gather(7, 0)
    for c in own_head:
        c.wait()

    for k in range(7):
        for c in range(2):
            for d in range(2):
                slab(k, d, c).wait_recv()
                if k < 6 or c == d:
                    slab(k + 1, d, c).start()
        for d in range(2):
            meta(k, d).wait_recv()
            if k < 6 or d == 0:
                meta(k + 1, d).start()
        for d in range(2):
            gather(k, d)
        if k == 1:
            for i in range(2):
                block(1, i).wait()
                block(2, i).start()
        if k == 2:
            send_round((0,))
        if k == 3:
            for i in range(2):
                block(2, i).wait()
                block(3, i).start()
            stats((0,))
        if k == 4:
            send_round((1, 2))
        if k == 5:
            for i in range(2):
                block(3, i).wait()
            send_round((3, 4))
        if k == 6:
            send_round((5,))
            stats((1, 2))

    slab(7, 0, 0).wait_recv()
    slab(7, 1, 1).wait_recv()
    meta(7, 0).wait_recv()
    gather(7, 1)
    send_round((6,))
    stats((3, 4))
    for k in range(6):
        turn(k)
        report(k).start()
    stats((5,))
    turn(6)
    report(6).start()
    stats((6,))
    turn(7)

    @pl.when(my_d == 0)
    def _():
        Rr[7] = Rs[7]

    @pl.when(my_d == 1)
    def _():
        report(7).start()

    for k in range(7):
        report(k).wait_recv()
        collect(k, jnp.where(my_d == 0, k + 1, -(k + 1)))

    @pl.when(my_d == 1)
    def _():
        report(7).wait()

    collect(7, jnp.where(my_d == 0, 0, -8))

    peak, mass, goal = (acc[4 * q : 4 * q + 4] for q in range(3))
    have = mass > 0.5
    largest = jnp.max(jnp.where(have, peak, -1e30), axis=0, keepdims=True)
    weight = jnp.where(have, jnp.exp(jnp.where(have, peak - largest, 0.0)), 0.0)
    E[0] = jnp.concatenate(
        [
            largest,
            jnp.sum(mass * weight, axis=0, keepdims=True),
            jnp.sum(goal, axis=0, keepdims=True),
            jnp.zeros((5, TOK), F32),
        ],
        axis=0,
    )

    def share(rel):
        return push(E.at[0], E.at[rel], es.at[rel], er.at[rel], lax.rem(seg + rel, 8), v)

    for rel in range(1, 8):
        share(rel).start()
    for rel in range(1, 8):
        share(rel).wait_recv()
    top = E[0, 0:1]
    for rel in range(1, 8):
        top = jnp.maximum(top, E[rel, 0:1])
    mass = jnp.zeros((1, TOK), F32)
    goal = jnp.zeros((1, TOK), F32)
    for rel in range(8):
        mass = mass + E[rel, 1:2] * jnp.exp(E[rel, 0:1] - top)
        goal = goal + E[rel, 2:3]
    out[...] = goal - (top + jnp.log(mass))

    for rel in range(1, 8):
        share(rel).wait_send()
        square(rel).wait_send()
    for k in range(8):
        for d in range(2):
            for c in range(2):
                if k < 7 or c == d:
                    slab(k, d, c).wait_send()
            if k < 7 or d == 0:
                meta(k, d).wait_send()
    for k in range(7):
        report(k).wait_send()
    for r in range(len(ROUNDS)):

        def left_here(rel, carry, r=r):
            partial(r, rel).wait_send()
            return carry

        lax.fori_loop(1, 8, left_here, 0)


def per_device(hidden, norm_gain, head, allowed, target_slot, target_offset):
    vmem = pl.BlockSpec(memory_space=pltpu.VMEM)
    hbm = pl.BlockSpec(memory_space=pl.ANY)
    dma = pltpu.SemaphoreType.DMA
    out = pl.pallas_call(
        kernel,
        out_shape=jax.ShapeDtypeStruct((1, TOK), F32),
        in_specs=[hbm, vmem, hbm, vmem, vmem, vmem],
        out_specs=vmem,
        scratch_shapes=[
            pltpu.VMEM((2, 8, TOK, SLAB), BF16),
            pltpu.VMEM((2, 8, 8, TOK), F32),
            pltpu.VMEM((4, 2, BLOCK, SLAB), BF16),
            pltpu.VMEM((4, 2, 8, 2, CAP, SLAB), BF16),
            pltpu.VMEM((8, 8, 4, CAP, 256), BF16),
            pltpu.VMEM((8, 8, 4, CAP, 256), BF16),
            pltpu.VMEM((8, 64, 128), F32),
            pltpu.VMEM((8, 8, 128), F32),
            pltpu.VMEM((8, 8, 128), F32),
            pltpu.VMEM((2, 64, TOK), F32),
            pltpu.VMEM((8, 8, TOK), F32),
            pltpu.VMEM((8, 8, TOK), F32),
            pltpu.VMEM((16, TOK), F32),
            dma((2, 8, 2)),
            dma((2, 8, 2)),
            dma((2, 8)),
            dma((2, 8)),
            dma((4, 2)),
            dma((4, 2)),
            dma((len(ROUNDS), 8)),
            dma((len(ROUNDS), 8)),
            dma((8,)),
            dma((8,)),
            dma((8,)),
            dma((8,)),
            dma((8,)),
            dma((8,)),
            dma((3,)),
        ],
        compiler_params=pltpu.CompilerParams(
            collective_id=0, has_side_effects=True, vmem_limit_bytes=56 * 2**20
        ),
    )(
        hidden,
        norm_gain.reshape(1, SLAB),
        head,
        allowed,
        target_slot.reshape(1, TOK),
        target_offset.reshape(1, TOK),
    )
    return out.reshape(TOK)


def solution(mesh):
    return jax.shard_map(
        per_device,
        mesh=mesh,
        in_specs=(
            P("vocab", "segment"),
            P("segment"),
            P("vocab", "segment"),
            P(None, "vocab"),
            P("vocab"),
            P("vocab"),
        ),
        out_specs=P("vocab"),
        check_vma=False,
    )
```

```python
import functools

import jax
import jax.numpy as jnp
from jax import lax
from jax.experimental import pallas as pl
from jax.experimental.pallas import tpu as pltpu
from jax.sharding import PartitionSpec as P

D = 8192
BLOCK = 512
A = 4
CAP = 16
NZ = 16
NX = 4
TOK = 256
SLAB = 1024
F32 = jnp.float32
BF16 = jnp.bfloat16
ROUND_A = ((0, 2, 1, 4, None), (0, 2, 0, 1, 0))
ROUND_B = ((0, 2, 4, 6, None), (2, 3, 1, 6, None), (2, 3, 0, 1, 0))
ROUND_C = ((0, 3, 6, 7, None), (3, 4, 1, 7, None), (3, 4, 0, 1, 0))
ROUND_D = ((0, 4, 7, 8, None),)
ROUND_E = ((0, 2, 0, 1, 1), (2, 4, 0, 1, 1))
ROUNDS = ROUND_A + ROUND_B + ROUND_C + ROUND_D + ROUND_E


def kernel(
    hid,
    gain,
    head,
    allowed,
    tslot,
    toff,
    out,
    X,
    F,
    N,
    Z,
    M,
    H,
    G,
    Pp,
    Pr,
    St,
    Rs,
    Rr,
    rcode,
    Sx,
    E,
    acc,
    xs,
    xr,
    fs,
    fr,
    ms,
    mr,
    hs,
    hr,
    ps,
    pr,
    ss,
    sr,
    es,
    er,
    ts,
    tr,
    own,
):
    seg = lax.axis_index("segment")
    v = lax.axis_index("vocab")
    z = v // NX
    x = lax.rem(v, NX)
    my_i = seg // 4
    my_h = lax.rem(seg // 2, 2)
    my_d = lax.rem(seg, 2)

    def at_z(step):
        return lax.rem(z + step + NZ, NZ) * NX + x

    def at_x(step):
        return z * NX + lax.rem(x + step + NX, NX)

    def push(src, dst, send, recv, s, d):
        return pltpu.make_async_remote_copy(
            src_ref=src,
            dst_ref=dst,
            send_sem=send,
            recv_sem=recv,
            device_id=(s, d),
            device_id_type=pl.DeviceIdType.MESH,
        )

    own_slab = pltpu.make_async_copy(hid, X.at[0, 0], own.at[0])
    own_slab.start()
    own_head = [
        pltpu.make_async_copy(head.at[pl.ds(i * BLOCK, BLOCK)], H.at[0, i], own.at[1 + i])
        for i in range(2)
    ]
    for c in own_head:
        c.start()

    barrier = pltpu.get_barrier_semaphore()
    for d in (at_z(1), at_z(-1), at_x(1), at_x(-1)):
        pl.semaphore_signal(
            barrier, inc=1, device_id=(seg, d), device_id_type=pl.DeviceIdType.MESH
        )
    for rel in range(1, 8):
        pl.semaphore_signal(
            barrier,
            inc=1,
            device_id=(lax.rem(seg + rel, 8), v),
            device_id_type=pl.DeviceIdType.MESH,
        )
    pl.semaphore_wait(barrier, 11)

    half = TOK // 2
    sides = (at_z(1), at_z(-1))

    def slab(k, d, c):
        rows = pl.ds(c * half, half)
        src = hid.at[rows] if k == 1 else X.at[d, k - 1, rows]
        return push(
            src, X.at[d, k, rows], xs.at[d, k, c], xr.at[d, k, c], seg, sides[d]
        )

    def far(n, d):
        src = (F.at[d, 0:64], F.at[d, 64:192], N.at[d, 0:64])[n]
        dst = (N.at[d, 0:64], N.at[d, 64:192], Z.at[d])[n]
        return push(src, dst, fs.at[d, n], fr.at[d, n], seg, sides[d])

    def meta(k, d):
        src = M.at[0, 0] if k == 1 else M.at[d, k - 1]
        dst = M.at[1, 0] if k == 8 else M.at[d, k]
        return push(src, dst, ms.at[d, k - 1], mr.at[d, k - 1], seg, sides[d])

    for c in range(2):
        for d in range(2):
            slab(1, d, c).start()

    first, second = head.at[pl.ds(0, BLOCK)], head.at[pl.ds(BLOCK, BLOCK)]

    def block(w, i):
        src = ((first, second), (second, first), (H.at[1, 0], H.at[1, 1]))[w - 1][i]
        return push(src, H.at[w, i], hs.at[w, i], hr.at[w, i], seg, at_x(1 - 2 * i))

    for i in range(2):
        block(1, i).start()

    tokens = lax.broadcasted_iota(jnp.int32, (TOK, TOK), 0)
    later = lax.broadcasted_iota(jnp.int32, (TOK, TOK), 1)
    upper = jnp.where(tokens < later, 1.0, 0.0).astype(BF16)
    blocks = lax.broadcasted_iota(jnp.int32, (128, TOK), 0)
    seen = jnp.zeros((128, 1), F32)
    codes = []
    for j in range(A):
        named = blocks == allowed[pl.ds(j, 1), :]
        hot = jnp.where(named, 1.0, 0.0)
        before = jnp.dot(hot.astype(BF16), upper, preferred_element_type=F32) + seen
        place = jnp.sum(jnp.where(named, before, 0.0), axis=0, keepdims=True)
        codes.append((allowed[pl.ds(j, 1), :] * CAP).astype(F32) + place)
        seen = seen + jnp.sum(hot, axis=1, keepdims=True)
    target = codes[0]
    for j in range(1, A):
        target = jnp.where(tslot[...] == j, codes[j], target)
    offset = toff[...].astype(F32)

    slot = lax.broadcasted_iota(jnp.int32, (CAP, TOK), 0)
    left, right, across = (lax.rem(x + s, NX) for s in (3, 1, 2))
    for i in range(2):
        for w in range(4):
            column = (x, (left, right)[i], (left, right)[i], across)[w]
            odd = (i, i, 1 - i, i)[w]
            which = (z * 8 + column * 2 + odd) * CAP
            rcode[i, pl.ds(w * CAP, CAP), :] = (slot + which).astype(F32)

    own_slab.wait()
    squares = jnp.zeros((TOK, 128), F32)
    for c in range(SLAB // 128):
        part = X[0, 0, :, pl.ds(c * 128, 128)].astype(F32)
        squares = squares + part * part
    Sx[0] = jnp.sum(squares.T.reshape(16, 8, TOK), axis=0)

    def square(rel):
        return push(
            Sx.at[0], Sx.at[rel], ss.at[rel], sr.at[rel], lax.rem(seg + rel, 8), v
        )

    for rel in range(1, 8):
        square(rel).start()
    total = Sx[0]
    for rel in range(1, 8):
        square(rel).wait_recv()
        total = total + Sx[rel]
    scale = lax.rsqrt(jnp.sum(total, axis=0, keepdims=True) * (1.0 / D) + 1e-05)
    M[0, 0] = jnp.concatenate(codes + [scale, target, offset, offset], axis=0)
    for d in range(2):
        meta(1, d).start()

    def hits(info, i, step):
        rows = rcode[i]
        if step is not None:
            rows = rows + ((lax.rem(z + step + NZ, NZ) - z) * 128).astype(F32)
        hit = rows == info[0:1, :]
        for j in range(1, A):
            hit = hit | (rows == info[j : j + 1, :])
        return hit

    def choose(hit):
        return jnp.where(hit, 1.0, 0.0).astype(BF16)

    def keep(k, d, i, info, hit, picked):
        size = jnp.sum(jnp.where(hit, info[4:5, :], 0.0), axis=1, keepdims=True)
        normed = (picked * size * gain[...]).astype(BF16)
        for w in range(4):
            G[w, i, k, d] = normed[w * CAP : (w + 1) * CAP]

    def gather(k, d):
        info = M[d, k]
        for i in range(2):
            hit = hits(info, i, None)
            picked = jnp.dot(choose(hit), X[d, k], preferred_element_type=F32)
            keep(k, d, i, info, hit, picked)

    def compact(d):
        info = M[d, 6]
        step = 1 - 2 * d
        pick = jnp.concatenate(
            [
                choose(hits(info, d, 2 * step)),
                choose(hits(info, 0, step)),
                choose(hits(info, 1, step)),
            ],
            axis=0,
        )
        F[d] = jnp.dot(pick, X[d, 6], preferred_element_type=F32).astype(BF16)

    def arrived(k, d, i, rows):
        info = M[d, k]
        keep(k, d, i, info, hits(info, i, None), rows.astype(F32))

    def spread(w, i, k0, count, logits):
        for d in range(2):
            for h in range(2):
                Pp[4 * i + 2 * h + d, pl.ds(k0, count), w] = logits[
                    :, d, :, 256 * h : 256 * (h + 1)
                ]

    def multiply(rows, w, i):
        return lax.dot_general(
            rows, H[w, i], (((1,), (1,)), ((), ())), preferred_element_type=F32
        )

    def products(w0, w1, k0, k1):
        count = k1 - k0

        def one(n, carry):
            w, i = n // 2, lax.rem(n, 2)
            rows = G[w, i, pl.ds(k0, count)].reshape(count * 2 * CAP, SLAB)
            logits = multiply(rows, w, i).reshape(count, 2, CAP, BLOCK).astype(BF16)
            spread(w, i, k0, count, logits)
            return carry

        lax.fori_loop(2 * w0, 2 * w1, one, 0)

    def products_flat(w0, w1, k):
        for w in range(w0, w1):
            for i in range(2):
                logits = multiply(G[w, i, k].reshape(2 * CAP, SLAB), w, i)
                spread(w, i, k, 1, logits.reshape(1, 2, CAP, BLOCK).astype(BF16))

    def products_last(w0, w1):
        for w in range(w0, w1):
            for i in range(2):
                logits = multiply(G[w, i, 0, 1], w, i).astype(BF16)
                for h in range(2):
                    Pp[4 * i + 2 * h + 1, 0, w] = logits[:, 256 * h : 256 * (h + 1)]

    def partial(r, rel):
        w0, w1, k0, k1, _ = ROUNDS[r]
        dest = lax.rem(seg + rel, 8)
        part = (pl.ds(k0, k1 - k0), pl.ds(w0, w1 - w0))
        return push(
            Pp.at[(dest, *part)],
            Pr.at[(rel, *part)],
            ps.at[r, rel],
            pr.at[r, rel],
            dest,
            v,
        )

    def each_peer(r, act):
        side = ROUNDS[r][4]

        def one(rel, carry):
            if side is None:
                act(partial(r, rel))
            else:

                @pl.when(lax.rem(seg + rel, 2) == side)
                def _():
                    act(partial(r, rel))

            return carry

        lax.fori_loop(1, 8, one, 0)

    def send(rounds):
        for r in rounds:
            each_peer(r, lambda copy: copy.start())

    def sent(rounds):
        for r in rounds:
            each_peer(r, lambda copy: copy.wait_send())

    def stats(rounds):
        for r in rounds:
            side = ROUNDS[r][4]
            if side is None:
                stats_of(r)
            else:
                pl.when(my_d == side)(functools.partial(stats_of, r))

    def stats_of(r):
        w0, w1, k0, k1, _ = ROUNDS[r]
        n = (w1 - w0) * CAP

        def arrive(rel, carry):
            partial(r, rel).wait_recv()
            return carry

        lax.fori_loop(1, 8, arrive, 0)

        def one(k, carry):
            span = pl.ds(w0, w1 - w0)
            logits = Pp[seg, k, span].reshape(n, 256).astype(F32)
            for rel in range(1, 8):
                logits = logits + Pr[rel, k, span].reshape(n, 256).astype(F32)
            info = M[my_d, k]
            rows = rcode[my_i, pl.ds(w0 * CAP, n), :]
            wanted = jnp.sum(
                jnp.where(rows == info[5:6, :], info[6:7, :] + 1.0, 0.0),
                axis=1,
                keepdims=True,
            )
            column = lax.broadcasted_iota(jnp.int32, (n, 256), 1) + 256 * my_h + 1
            peak = jnp.max(logits, axis=1, keepdims=True)
            mass = jnp.sum(jnp.exp(logits - peak), axis=1, keepdims=True)
            goal = jnp.sum(
                jnp.where(column.astype(F32) == wanted, logits, 0.0),
                axis=1,
                keepdims=True,
            )
            lane = lax.broadcasted_iota(jnp.int32, (n, 128), 1)
            St[k, pl.ds(w0 * CAP, n), :] = jnp.where(
                lane == 0, peak, jnp.where(lane == 1, mass, goal)
            )
            return carry

        if k1 - k0 == 1:
            one(k0, 0)
        else:
            lax.fori_loop(k0, k1, one, 0)

    def report(k):
        step = jnp.where(my_d == 0, -k, k) if k else 8
        return push(Rs.at[k], Rr.at[k], ts.at[k], tr.at[k], seg, at_z(step))

    def turn(k):
        rows = St[k]
        Rs[k] = jnp.concatenate([rows, rows], axis=0).T[0:8]

    acc[...] = jnp.zeros((16, TOK), F32)

    def collect(k, step):
        plane = lax.rem(z + step + NZ, NZ) - z
        rows = rcode[my_i] + (plane * 128).astype(F32)
        columns = jnp.concatenate([Rr[k]] * 16, axis=0).T
        for j in range(A):
            match = rows == M[0, 0, j : j + 1, :]
            for q in range(3):
                acc[pl.ds(4 * q + j, 1), :] += jnp.sum(
                    jnp.where(match, columns[0:64, q : q + 1], 0.0), axis=0, keepdims=True
                )

    gather(0, 0)
    for w in range(4):
        for i in range(2):
            G[w, i, 0, 1] = jnp.zeros((CAP, SLAB), BF16)
    for c in own_head:
        c.wait()

    for k in range(1, 6):
        for d in range(2):
            slab(k, d, 0).wait_recv()
            slab(k + 1, d, 0).start()
        for d in range(2):
            slab(k, d, 1).wait_recv()
            meta(k, d).wait_recv()
            meta(k + 1, d).start()
            slab(k + 1, d, 1).start()
        for d in range(2):
            gather(k, d)
        if k == 2:
            for i in range(2):
                block(1, i).wait()
                block(2, i).start()
        if k == 3:
            products(0, 2, 0, 4)
            send((0, 1))
        if k == 4:
            for i in range(2):
                block(2, i).wait()
                block(3, i).start()
        if k == 5:
            products(0, 2, 4, 6)
            send((2,))
            products(2, 3, 0, 6)
            send((3, 4))
            stats((0, 1))

    for d in range(2):
        slab(6, d, 0).wait_recv()
    for d in range(2):
        slab(6, d, 1).wait_recv()
        meta(6, d).wait_recv()
        meta(7, d).start()
        compact(d)
        far(0, d).start()
        far(1, d).start()
    for d in range(2):
        gather(6, d)
    products(0, 3, 6, 7)
    send((5,))
    for d in range(2):
        meta(7, d).wait_recv()
        far(0, d).wait_recv()
        if d == 0:
            meta(8, d).start()
        far(2, d).start()
    for i in range(2):
        block(3, i).wait()
    products(3, 4, 0, 7)
    send((6, 7))
    stats((2, 3, 4))

    for d in range(2):
        far(1, d).wait_recv()
        for i in range(2):
            arrived(7, d, i, N[d, 64 + 64 * i : 128 + 64 * i])
    products_flat(0, 4, 7)
    send((8,))

    meta(8, 0).wait_recv()
    for d in range(2):
        far(2, d).wait_recv()
        arrived(0, 1, d, Z[d])
    products_last(0, 2)
    send((9,))
    products_last(2, 4)
    send((10,))

    stats((5, 6, 7))
    for k in range(1, 7):
        turn(k)
        report(k).start()
    stats((8,))
    turn(7)
    report(7).start()
    stats((9, 10))
    turn(0)

    @pl.when(my_d == 0)
    def _():
        Rr[0] = Rs[0]

    @pl.when(my_d == 1)
    def _():
        report(0).start()

    for k in range(1, 7):
        for d in range(2):
            for c in range(2):
                slab(k, d, c).wait_send()
    for k in range(1, 9):
        for d in range(2 if k < 8 else 1):
            meta(k, d).wait_send()
    for d in range(2):
        for n in range(3):
            far(n, d).wait_send()
    for rel in range(1, 8):
        square(rel).wait_send()
    sent(range(len(ROUNDS)))

    for k in range(1, 8):
        report(k).wait_recv()
        collect(k, jnp.where(my_d == 0, k, -k))

    @pl.when(my_d == 1)
    def _():
        report(0).wait_recv()

    collect(0, jnp.where(my_d == 0, 0, -8))

    peak, mass, goal = (acc[4 * q : 4 * q + 4] for q in range(3))
    have = mass > 0.5
    largest = jnp.max(jnp.where(have, peak, -1e30), axis=0, keepdims=True)
    weight = jnp.where(have, jnp.exp(jnp.where(have, peak - largest, 0.0)), 0.0)
    E[0] = jnp.concatenate(
        [
            largest,
            jnp.sum(mass * weight, axis=0, keepdims=True),
            jnp.sum(goal, axis=0, keepdims=True),
            jnp.zeros((5, TOK), F32),
        ],
        axis=0,
    )

    def share(rel):
        return push(E.at[0], E.at[rel], es.at[rel], er.at[rel], lax.rem(seg + rel, 8), v)

    for rel in range(1, 8):
        share(rel).start()
    for k in range(1, 8):
        report(k).wait_send()

    @pl.when(my_d == 1)
    def _():
        report(0).wait_send()

    for rel in range(1, 8):
        share(rel).wait_recv()
    top = E[0, 0:1]
    for rel in range(1, 8):
        top = jnp.maximum(top, E[rel, 0:1])
    mass = jnp.zeros((1, TOK), F32)
    goal = jnp.zeros((1, TOK), F32)
    for rel in range(8):
        mass = mass + E[rel, 1:2] * jnp.exp(E[rel, 0:1] - top)
        goal = goal + E[rel, 2:3]
    out[...] = goal - (top + jnp.log(mass))
    for rel in range(1, 8):
        share(rel).wait_send()


def per_device(hidden, norm_gain, head, allowed, target_slot, target_offset):
    vmem = pl.BlockSpec(memory_space=pltpu.VMEM)
    hbm = pl.BlockSpec(memory_space=pl.ANY)
    dma = pltpu.SemaphoreType.DMA
    out = pl.pallas_call(
        kernel,
        out_shape=jax.ShapeDtypeStruct((1, TOK), F32),
        in_specs=[hbm, vmem, hbm, vmem, vmem, vmem],
        out_specs=vmem,
        scratch_shapes=[
            pltpu.VMEM((2, 7, TOK, SLAB), BF16),
            pltpu.VMEM((2, 192, SLAB), BF16),
            pltpu.VMEM((2, 192, SLAB), BF16),
            pltpu.VMEM((2, 64, SLAB), BF16),
            pltpu.VMEM((2, 8, 8, TOK), F32),
            pltpu.VMEM((4, 2, BLOCK, SLAB), BF16),
            pltpu.VMEM((4, 2, 8, 2, CAP, SLAB), BF16),
            pltpu.VMEM((8, 8, 4, CAP, 256), BF16),
            pltpu.VMEM((8, 8, 4, CAP, 256), BF16),
            pltpu.VMEM((8, 64, 128), F32),
            pltpu.VMEM((8, 8, 128), F32),
            pltpu.VMEM((8, 8, 128), F32),
            pltpu.VMEM((2, 64, TOK), F32),
            pltpu.VMEM((8, 8, TOK), F32),
            pltpu.VMEM((8, 8, TOK), F32),
            pltpu.VMEM((16, TOK), F32),
            dma((2, 7, 2)),
            dma((2, 7, 2)),
            dma((2, 3)),
            dma((2, 3)),
            dma((2, 8)),
            dma((2, 8)),
            dma((4, 2)),
            dma((4, 2)),
            dma((len(ROUNDS), 8)),
            dma((len(ROUNDS), 8)),
            dma((8,)),
            dma((8,)),
            dma((8,)),
            dma((8,)),
            dma((8,)),
            dma((8,)),
            dma((3,)),
        ],
        compiler_params=pltpu.CompilerParams(
            collective_id=0, has_side_effects=True, vmem_limit_bytes=56 * 2**20
        ),
    )(
        hidden,
        norm_gain.reshape(1, SLAB),
        head,
        allowed,
        target_slot.reshape(1, TOK),
        target_offset.reshape(1, TOK),
    )
    return out.reshape(TOK)


def solution(mesh):
    return jax.shard_map(
        per_device,
        mesh=mesh,
        in_specs=(
            P("vocab", "segment"),
            P("segment"),
            P("vocab", "segment"),
            P(None, "vocab"),
            P("vocab"),
            P("vocab"),
        ),
        out_specs=P("vocab"),
        check_vma=False,
    )
```

```python
import functools

import jax
import jax.numpy as jnp
from jax import lax
from jax.experimental import pallas as pl
from jax.experimental.pallas import tpu as pltpu
from jax.sharding import PartitionSpec as P

D = 8192
BLOCK = 512
A = 4
CAP = 16
NZ = 16
NX = 4
TOK = 256
SLAB = 1024
F32 = jnp.float32
BF16 = jnp.bfloat16
ROUND_A = ((0, 2, 1, 4, None), (0, 2, 0, 1, 0))
ROUND_B = ((0, 2, 4, 6, None), (2, 3, 1, 6, None), (2, 3, 0, 1, 0))
ROUND_C = ((0, 3, 6, 7, None), (3, 4, 1, 7, None), (3, 4, 0, 1, 0))
ROUND_D = ((0, 4, 7, 8, None),)
ROUND_E = ((0, 2, 0, 1, 1), (2, 4, 0, 1, 1))
ROUNDS = ROUND_A + ROUND_B + ROUND_C + ROUND_D + ROUND_E


def kernel(
    hid,
    gain,
    head,
    allowed,
    tslot,
    toff,
    out,
    X,
    XS,
    Z,
    M,
    MS,
    H,
    G,
    Pp,
    Pr,
    St,
    Rs,
    Rr,
    Qs,
    Qr,
    rcode,
    Sx,
    E,
    acc,
    xs,
    xr,
    ms,
    mr,
    hs,
    hr,
    ps,
    pr,
    ss,
    sr,
    es,
    er,
    ts,
    tr,
    qs,
    qr,
    own,
):
    seg = lax.axis_index("segment")
    v = lax.axis_index("vocab")
    z = v // NX
    x = lax.rem(v, NX)
    my_i = seg // 4
    my_h = lax.rem(seg // 2, 2)
    my_d = lax.rem(seg, 2)

    def at_z(step):
        return lax.rem(z + step + NZ, NZ) * NX + x

    def at_x(step):
        return z * NX + lax.rem(x + step + NX, NX)

    def push(src, dst, send, recv, s, d):
        return pltpu.make_async_remote_copy(
            src_ref=src,
            dst_ref=dst,
            send_sem=send,
            recv_sem=recv,
            device_id=(s, d),
            device_id_type=pl.DeviceIdType.MESH,
        )

    own_slab = pltpu.make_async_copy(hid, X.at[0, 0], own.at[0])
    own_slab.start()
    own_head = [
        pltpu.make_async_copy(head.at[pl.ds(i * BLOCK, BLOCK)], H.at[0, i], own.at[1 + i])
        for i in range(2)
    ]
    for c in own_head:
        c.start()

    barrier = pltpu.get_barrier_semaphore()
    for d in (at_z(1), at_z(-1), at_x(1), at_x(-1)):
        pl.semaphore_signal(
            barrier, inc=1, device_id=(seg, d), device_id_type=pl.DeviceIdType.MESH
        )
    for rel in range(1, 8):
        pl.semaphore_signal(
            barrier,
            inc=1,
            device_id=(lax.rem(seg + rel, 8), v),
            device_id_type=pl.DeviceIdType.MESH,
        )
    tokens = lax.broadcasted_iota(jnp.int32, (TOK, TOK), 0)
    later = lax.broadcasted_iota(jnp.int32, (TOK, TOK), 1)
    upper = jnp.where(tokens < later, 1.0, 0.0).astype(BF16)
    blocks = lax.broadcasted_iota(jnp.int32, (128, TOK), 0)
    seen = jnp.zeros((128, 1), F32)
    codes = []
    for j in range(A):
        named = blocks == allowed[pl.ds(j, 1), :]
        hot = jnp.where(named, 1.0, 0.0)
        before = jnp.dot(hot.astype(BF16), upper, preferred_element_type=F32) + seen
        place = jnp.sum(jnp.where(named, before, 0.0), axis=0, keepdims=True)
        codes.append((allowed[pl.ds(j, 1), :] * CAP).astype(F32) + place)
        seen = seen + jnp.sum(hot, axis=1, keepdims=True)
    target = codes[0]
    for j in range(1, A):
        target = jnp.where(tslot[...] == j, codes[j], target)
    offset = toff[...].astype(F32)

    slot = lax.broadcasted_iota(jnp.int32, (CAP, TOK), 0)
    left, right, across = (lax.rem(x + s, NX) for s in (3, 1, 2))
    for i in range(2):
        for w in range(4):
            column = (x, (left, right)[i], (left, right)[i], across)[w]
            odd = (i, i, 1 - i, i)[w]
            which = (z * 8 + column * 2 + odd) * CAP
            rcode[i, pl.ds(w * CAP, CAP), :] = (slot + which).astype(F32)

    def hits(info, i, step):
        rows = rcode[i]
        if step is not None:
            rows = rows + ((lax.rem(z + step + NZ, NZ) - z) * 128).astype(F32)
        hit = rows == info[0:1, :]
        for j in range(1, A):
            hit = hit | (rows == info[j : j + 1, :])
        return hit

    def choose(hit):
        return jnp.where(hit, 1.0, 0.0).astype(BF16)

    named = jnp.concatenate(codes, axis=0)
    own_slab.wait()
    picks = []
    for d in range(2):
        step = 1 - 2 * d

        def marked(hit):
            return jnp.max(jnp.where(hit, 1.0, 0.0), axis=0, keepdims=True)

        last = marked(hits(named, d, 8))
        near = jnp.maximum(
            marked(hits(named, 0, 7 * step)), marked(hits(named, 1, 7 * step))
        )
        near = near * (1.0 - last)
        rest = 1.0 - last - near
        classes = jnp.concatenate([last, near, rest, jnp.zeros((13, TOK), F32)], axis=0)
        rank = jnp.dot(classes.astype(BF16), upper, preferred_element_type=F32)
        n_last = jnp.sum(last, axis=1, keepdims=True)
        n_near = jnp.sum(near, axis=1, keepdims=True)
        position = (
            last * rank[0:1]
            + near * (n_last + rank[1:2])
            + rest * (n_last + n_near + rank[2:3])
        )
        pick = jnp.where(tokens.astype(F32) == position, 1.0, 0.0)
        picks.append(pick)
        for c in range(2):
            rows = slice(c * 128, (c + 1) * 128)
            XS[d, rows] = jnp.dot(
                pick[rows].astype(BF16), X[0, 0], preferred_element_type=F32
            ).astype(BF16)
    for d in range(2):
        X[d, 7, 192:256] = jnp.zeros((64, SLAB), BF16)
        Z[d, 64:128] = jnp.zeros((64, SLAB), BF16)

    pl.semaphore_wait(barrier, 11)

    sides = (at_z(1), at_z(-1))

    def slab(k, d, c):
        begin, size = ((0, 64), (64, 64), (128, 64))[c] if k == 7 else (c * 128, 128)
        if k == 8:
            begin, size = 0, 64
        rows = pl.ds(begin, size)
        src = XS.at[d, rows] if k == 1 else X.at[d, k - 1, rows]
        dst = Z.at[d, rows] if k == 8 else X.at[d, k, rows]
        return push(src, dst, xs.at[d, k, c], xr.at[d, k, c], seg, sides[d])

    def meta(k, d):
        src = MS.at[d] if k == 1 else M.at[d, k - 1]
        return push(src, M.at[d, k], ms.at[d, k], mr.at[d, k], seg, sides[d])

    for c in range(2):
        for d in range(2):
            slab(1, d, c).start()

    first, second = head.at[pl.ds(0, BLOCK)], head.at[pl.ds(BLOCK, BLOCK)]

    def block(w, i):
        src = ((first, second), (second, first), (H.at[1, 0], H.at[1, 1]))[w - 1][i]
        return push(src, H.at[w, i], hs.at[w, i], hr.at[w, i], seg, at_x(1 - 2 * i))

    for i in range(2):
        block(1, i).start()

    squares = jnp.zeros((TOK, 128), F32)
    for c in range(SLAB // 128):
        part = X[0, 0, :, pl.ds(c * 128, 128)].astype(F32)
        squares = squares + part * part
    Sx[0] = jnp.sum(squares.T.reshape(16, 8, TOK), axis=0)

    def square(rel):
        return push(
            Sx.at[0], Sx.at[rel], ss.at[rel], sr.at[rel], lax.rem(seg + rel, 8), v
        )

    for rel in range(1, 8):
        square(rel).start()
    total = Sx[0]
    for rel in range(1, 8):
        square(rel).wait_recv()
        total = total + Sx[rel]
    scale = lax.rsqrt(jnp.sum(total, axis=0, keepdims=True) * (1.0 / D) + 1e-05)
    info = jnp.concatenate(codes + [scale, target, offset, offset], axis=0)
    M[0, 0] = info
    for d in range(2):
        MS[d] = lax.dot_general(
            info,
            picks[d],
            (((1,), (1,)), ((), ())),
            precision=lax.Precision.HIGHEST,
            preferred_element_type=F32,
        )
        meta(1, d).start()

    def keep(k, d, i, info, hit, picked):
        size = jnp.sum(jnp.where(hit, info[4:5, :], 0.0), axis=1, keepdims=True)
        normed = (picked * size * gain[...]).astype(BF16)
        for w in range(4):
            G[w, i, k, d] = normed[w * CAP : (w + 1) * CAP]

    def gather(k, d):
        info = M[d, k]
        for i in range(2):
            hit = hits(info, i, None)
            picked = jnp.dot(choose(hit), X[d, k], preferred_element_type=F32)
            keep(k, d, i, info, hit, picked)

    def gather_last():
        for i in range(2):
            info = M[i, 8]
            hit = hits(info, i, None)
            picked = jnp.dot(choose(hit)[:, 0:128], Z[i], preferred_element_type=F32)
            keep(0, 1, i, info, hit, picked)

    def spread(w, i, k0, count, logits):
        for d in range(2):
            for h in range(2):
                Pp[4 * i + 2 * h + d, pl.ds(k0, count), w] = logits[
                    :, d, :, 256 * h : 256 * (h + 1)
                ]

    def multiply(rows, w, i):
        return lax.dot_general(
            rows, H[w, i], (((1,), (1,)), ((), ())), preferred_element_type=F32
        )

    def products(w0, w1, k0, k1):
        count = k1 - k0

        def one(n, carry):
            w, i = n // 2, lax.rem(n, 2)
            rows = G[w, i, pl.ds(k0, count)].reshape(count * 2 * CAP, SLAB)
            logits = multiply(rows, w, i).reshape(count, 2, CAP, BLOCK).astype(BF16)
            spread(w, i, k0, count, logits)
            return carry

        lax.fori_loop(2 * w0, 2 * w1, one, 0)

    def products_flat(w0, w1, k):
        for w in range(w0, w1):
            for i in range(2):
                logits = multiply(G[w, i, k].reshape(2 * CAP, SLAB), w, i)
                spread(w, i, k, 1, logits.reshape(1, 2, CAP, BLOCK).astype(BF16))

    def products_last(w0, w1):
        for w in range(w0, w1):
            for i in range(2):
                logits = multiply(G[w, i, 0, 1], w, i).astype(BF16)
                for h in range(2):
                    Pp[4 * i + 2 * h + 1, 0, w] = logits[:, 256 * h : 256 * (h + 1)]

    def partial(r, rel):
        w0, w1, k0, k1, _ = ROUNDS[r]
        dest = lax.rem(seg + rel, 8)
        part = (pl.ds(k0, k1 - k0), pl.ds(w0, w1 - w0))
        return push(
            Pp.at[(dest, *part)],
            Pr.at[(rel, *part)],
            ps.at[r, rel],
            pr.at[r, rel],
            dest,
            v,
        )

    def each_peer(r, act):
        side = ROUNDS[r][4]

        def one(rel, carry):
            if side is None:
                act(partial(r, rel))
            else:

                @pl.when(lax.rem(seg + rel, 2) == side)
                def _():
                    act(partial(r, rel))

            return carry

        lax.fori_loop(1, 8, one, 0)

    def send(rounds):
        for r in rounds:
            each_peer(r, lambda copy: copy.start())

    def sent(rounds):
        for r in rounds:
            each_peer(r, lambda copy: copy.wait_send())

    def stats(rounds):
        for r in rounds:
            side = ROUNDS[r][4]
            if side is None:
                stats_of(r)
            else:
                pl.when(my_d == side)(functools.partial(stats_of, r))

    def stats_of(r):
        w0, w1, k0, k1, _ = ROUNDS[r]
        n = (w1 - w0) * CAP

        def arrive(rel, carry):
            partial(r, rel).wait_recv()
            return carry

        lax.fori_loop(1, 8, arrive, 0)

        last = r >= len(ROUNDS) - len(ROUND_E)

        def one(k, carry):
            span = pl.ds(w0, w1 - w0)
            logits = Pp[seg, k, span].reshape(n, 256).astype(F32)
            for rel in range(1, 8):
                logits = logits + Pr[rel, k, span].reshape(n, 256).astype(F32)
            info = M[my_i if last else my_d, 8 if last else k]
            rows = rcode[my_i, pl.ds(w0 * CAP, n), :]
            wanted = jnp.sum(
                jnp.where(rows == info[5:6, :], info[6:7, :] + 1.0, 0.0),
                axis=1,
                keepdims=True,
            )
            column = lax.broadcasted_iota(jnp.int32, (n, 256), 1) + 256 * my_h + 1
            peak = jnp.max(logits, axis=1, keepdims=True)
            mass = jnp.sum(jnp.exp(logits - peak), axis=1, keepdims=True)
            goal = jnp.sum(
                jnp.where(column.astype(F32) == wanted, logits, 0.0),
                axis=1,
                keepdims=True,
            )
            lane = lax.broadcasted_iota(jnp.int32, (n, 128), 1)
            St[k, pl.ds(w0 * CAP, n), :] = jnp.where(
                lane == 0, peak, jnp.where(lane == 1, mass, goal)
            )
            return carry

        if k1 - k0 == 1:
            one(k0, 0)
        else:
            lax.fori_loop(k0, k1, one, 0)

    def report(k):
        step = jnp.where(my_d == 0, -k, k)
        return push(Rs.at[k], Rr.at[k], ts.at[k], tr.at[k], seg, at_z(step))

    def turn(k):
        rows = St[k]
        Rs[k] = jnp.concatenate([rows, rows], axis=0).T[0:8]

    acc[...] = jnp.zeros((16, TOK), F32)

    def collect(k, step):
        plane = lax.rem(z + step + NZ, NZ) - z
        rows = rcode[my_i] + (plane * 128).astype(F32)
        columns = jnp.concatenate([Rr[k]] * 16, axis=0).T
        for j in range(A):
            match = rows == M[0, 0, j : j + 1, :]
            for q in range(3):
                acc[pl.ds(4 * q + j, 1), :] += jnp.sum(
                    jnp.where(match, columns[0:64, q : q + 1], 0.0), axis=0, keepdims=True
                )

    gather(0, 0)
    for w in range(4):
        for i in range(2):
            G[w, i, 0, 1] = jnp.zeros((CAP, SLAB), BF16)
    for c in own_head:
        c.wait()

    for k in range(1, 6):
        for d in range(2):
            slab(k, d, 0).wait_recv()
            slab(k + 1, d, 0).start()
        for d in range(2):
            slab(k, d, 1).wait_recv()
            meta(k, d).wait_recv()
            meta(k + 1, d).start()
            slab(k + 1, d, 1).start()
        for d in range(2):
            gather(k, d)
        if k == 2:
            for i in range(2):
                block(1, i).wait()
                block(2, i).start()
        if k == 3:
            products(0, 2, 0, 4)
            send((0, 1))
        if k == 4:
            for i in range(2):
                block(2, i).wait()
                block(3, i).start()
        if k == 5:
            products(0, 2, 4, 6)
            send((2,))
            products(2, 3, 0, 6)
            send((3, 4))
            stats((0, 1))

    for d in range(2):
        slab(6, d, 0).wait_recv()
        slab(7, d, 0).start()
        slab(7, d, 1).start()
    for d in range(2):
        slab(6, d, 1).wait_recv()
        meta(6, d).wait_recv()
        meta(7, d).start()
        slab(7, d, 2).start()
    for d in range(2):
        gather(6, d)
    products(0, 3, 6, 7)
    send((5,))
    for d in range(2):
        slab(7, d, 0).wait_recv()
        meta(7, d).wait_recv()
        meta(8, d).start()
        slab(8, d, 0).start()
    for i in range(2):
        block(3, i).wait()
    products(3, 4, 0, 7)
    send((6, 7))
    stats((2, 3, 4))

    for d in range(2):
        slab(7, d, 1).wait_recv()
        slab(7, d, 2).wait_recv()
    for d in range(2):
        gather(7, d)
    products_flat(0, 4, 7)
    send((8,))

    for d in range(2):
        slab(8, d, 0).wait_recv()
        meta(8, d).wait_recv()
    gather_last()
    products_last(0, 2)
    send((9,))
    products_last(2, 4)
    send((10,))

    stats((5, 6, 7))
    for k in range(1, 7):
        turn(k)
        report(k).start()
    stats((8,))
    turn(7)
    report(7).start()

    def finish(rel):
        return push(
            Qs, Qr.at[2 * my_i + my_h], qs.at[rel], qr.at[2 * my_i + my_h],
            lax.rem(seg + rel, 8), at_z(8),
        )

    @pl.when(my_d == 0)
    def _():
        turn(0)
        Rr[0] = Rs[0]

    stats((9, 10))

    @pl.when(my_d == 1)
    def _():
        rows = St[0]
        turned = jnp.concatenate([rows, rows], axis=0).T
        lane = lax.broadcasted_iota(jnp.int32, (1, 128), 1)
        Qs[...] = jnp.concatenate(
            [jnp.where(lane < 64, turned[0:1], turned[1:2]), turned[2:3]], axis=0
        )
        for rel in range(8):
            finish(rel).start()

    for k in range(1, 9):
        for d in range(2):
            for c in range(2 if k < 7 else (3, 1)[k - 7]):
                slab(k, d, c).wait_send()
            meta(k, d).wait_send()
    for rel in range(1, 8):
        square(rel).wait_send()
    sent(range(len(ROUNDS)))

    for k in range(1, 8):
        report(k).wait_recv()
        collect(k, jnp.where(my_d == 0, k, -k))

    @pl.when(my_d == 0)
    def _():
        collect(0, 0)

    peak, mass, goal = (acc[4 * q : 4 * q + 4] for q in range(3))
    have = mass > 0.5
    largest = jnp.max(jnp.where(have, peak, -1e30), axis=0, keepdims=True)
    weight = jnp.where(have, jnp.exp(jnp.where(have, peak - largest, 0.0)), 0.0)
    E[0] = jnp.concatenate(
        [
            largest,
            jnp.sum(mass * weight, axis=0, keepdims=True),
            jnp.sum(goal, axis=0, keepdims=True),
            jnp.zeros((5, TOK), F32),
        ],
        axis=0,
    )

    def share(rel):
        return push(E.at[0], E.at[rel], es.at[rel], er.at[rel], lax.rem(seg + rel, 8), v)

    for rel in range(1, 8):
        share(rel).start()
    for k in range(1, 8):
        report(k).wait_send()

    for rel in range(1, 8):
        share(rel).wait_recv()
    for n in range(4):
        push(Qs, Qr.at[n], qs.at[n], qr.at[n], seg, at_z(8)).wait_recv()

    stacked = jnp.concatenate([Qr[n] for n in range(4)], axis=0)
    columns = jnp.concatenate([stacked] * 16, axis=0).T
    last = []
    plane = ((lax.rem(z + 8, NZ) - z) * 128).astype(F32)
    for i in range(2):
        first, second = 4 * i, 4 * i + 2
        peaks = [columns[0:64, n : n + 1] for n in (first, second)]
        peak = jnp.maximum(peaks[0], peaks[1])
        mass = columns[64:128, first : first + 1] * jnp.exp(peaks[0] - peak)
        mass = mass + columns[64:128, second : second + 1] * jnp.exp(peaks[1] - peak)
        goal = columns[0:64, first + 1 : first + 2] + columns[0:64, second + 1 : second + 2]
        last.append((rcode[i] + plane, peak, mass, goal))
    found = []
    for j in range(A):
        rows = M[0, 0, j : j + 1, :]
        sums = [jnp.zeros((1, TOK), F32)] * 3
        for codes_of, *values in last:
            match = codes_of == rows
            sums = [
                s + jnp.sum(jnp.where(match, value, 0.0), axis=0, keepdims=True)
                for s, value in zip(sums, values)
            ]
        found.append(sums)

    top = E[0, 0:1]
    for rel in range(1, 8):
        top = jnp.maximum(top, E[rel, 0:1])
    for peak, mass, _ in found:
        top = jnp.maximum(top, jnp.where(mass > 0.5, peak, -1e30))
    mass = jnp.zeros((1, TOK), F32)
    goal = jnp.zeros((1, TOK), F32)
    for rel in range(8):
        mass = mass + E[rel, 1:2] * jnp.exp(E[rel, 0:1] - top)
        goal = goal + E[rel, 2:3]
    for a_peak, a_mass, a_goal in found:
        here = a_mass > 0.5
        weight = jnp.exp(jnp.where(here, a_peak - top, 0.0))
        mass = mass + jnp.where(here, a_mass * weight, 0.0)
        goal = goal + a_goal
    out[...] = goal - (top + jnp.log(mass))
    for rel in range(1, 8):
        share(rel).wait_send()

    @pl.when(my_d == 1)
    def _():
        for rel in range(8):
            finish(rel).wait_send()


def per_device(hidden, norm_gain, head, allowed, target_slot, target_offset):
    vmem = pl.BlockSpec(memory_space=pltpu.VMEM)
    hbm = pl.BlockSpec(memory_space=pl.ANY)
    dma = pltpu.SemaphoreType.DMA
    out = pl.pallas_call(
        kernel,
        out_shape=jax.ShapeDtypeStruct((1, TOK), F32),
        in_specs=[hbm, vmem, hbm, vmem, vmem, vmem],
        out_specs=vmem,
        scratch_shapes=[
            pltpu.VMEM((2, 8, TOK, SLAB), BF16),
            pltpu.VMEM((2, TOK, SLAB), BF16),
            pltpu.VMEM((2, 128, SLAB), BF16),
            pltpu.VMEM((2, 9, 8, TOK), F32),
            pltpu.VMEM((2, 8, TOK), F32),
            pltpu.VMEM((4, 2, BLOCK, SLAB), BF16),
            pltpu.VMEM((4, 2, 8, 2, CAP, SLAB), BF16),
            pltpu.VMEM((8, 8, 4, CAP, 256), BF16),
            pltpu.VMEM((8, 8, 4, CAP, 256), BF16),
            pltpu.VMEM((8, 64, 128), F32),
            pltpu.VMEM((8, 8, 128), F32),
            pltpu.VMEM((8, 8, 128), F32),
            pltpu.VMEM((2, 128), F32),
            pltpu.VMEM((4, 2, 128), F32),
            pltpu.VMEM((2, 64, TOK), F32),
            pltpu.VMEM((8, 8, TOK), F32),
            pltpu.VMEM((8, 8, TOK), F32),
            pltpu.VMEM((16, TOK), F32),
            dma((2, 9, 3)),
            dma((2, 9, 3)),
            dma((2, 9)),
            dma((2, 9)),
            dma((4, 2)),
            dma((4, 2)),
            dma((len(ROUNDS), 8)),
            dma((len(ROUNDS), 8)),
            dma((8,)),
            dma((8,)),
            dma((8,)),
            dma((8,)),
            dma((8,)),
            dma((8,)),
            dma((8,)),
            dma((4,)),
            dma((3,)),
        ],
        compiler_params=pltpu.CompilerParams(
            collective_id=0, has_side_effects=True, vmem_limit_bytes=56 * 2**20
        ),
    )(
        hidden,
        norm_gain.reshape(1, SLAB),
        head,
        allowed,
        target_slot.reshape(1, TOK),
        target_offset.reshape(1, TOK),
    )
    return out.reshape(TOK)


def solution(mesh):
    return jax.shard_map(
        per_device,
        mesh=mesh,
        in_specs=(
            P("vocab", "segment"),
            P("segment"),
            P("vocab", "segment"),
            P(None, "vocab"),
            P("vocab"),
            P("vocab"),
        ),
        out_specs=P("vocab"),
        check_vma=False,
    )
```

```python
import functools

import jax
import jax.numpy as jnp
from jax import lax
from jax.experimental import pallas as pl
from jax.experimental.pallas import tpu as pltpu
from jax.sharding import PartitionSpec as P

D = 8192
BLOCK = 512
A = 4
CAP = 16
NZ = 16
NX = 4
TOK = 256
SLAB = 1024
F32 = jnp.float32
BF16 = jnp.bfloat16
ROUND_A = ((0, 2, 1, 4, None), (0, 2, 0, 1, 0))
ROUND_B = ((0, 2, 4, 6, None), (2, 3, 1, 6, None), (2, 3, 0, 1, 0))
ROUND_C = ((0, 3, 6, 7, None), (3, 4, 1, 7, None), (3, 4, 0, 1, 0))
ROUND_D = ((0, 2, 7, 8, None), (2, 4, 7, 8, None))
ROUND_E = ((0, 2, 0, 1, 1), (2, 4, 0, 1, 1))
ROUNDS = ROUND_A + ROUND_B + ROUND_C + ROUND_D + ROUND_E


def kernel(
    hid,
    gain,
    head,
    allowed,
    tslot,
    toff,
    out,
    X,
    XS,
    Z,
    M,
    MS,
    H,
    G,
    Pp,
    Pr,
    St,
    Rs,
    Rr,
    Qs,
    Qr,
    table,
    rcode,
    Sx,
    E,
    acc,
    xs,
    xr,
    ms,
    mr,
    hs,
    hr,
    ps,
    pr,
    ss,
    sr,
    es,
    er,
    ts,
    tr,
    qs,
    qr,
    own,
):
    seg = lax.axis_index("segment")
    v = lax.axis_index("vocab")
    z = v // NX
    x = lax.rem(v, NX)
    my_i = seg // 4
    my_h = lax.rem(seg // 2, 2)
    my_d = lax.rem(seg, 2)

    def at_z(step):
        return lax.rem(z + step + NZ, NZ) * NX + x

    def at_x(step):
        return z * NX + lax.rem(x + step + NX, NX)

    def push(src, dst, send, recv, s, d):
        return pltpu.make_async_remote_copy(
            src_ref=src,
            dst_ref=dst,
            send_sem=send,
            recv_sem=recv,
            device_id=(s, d),
            device_id_type=pl.DeviceIdType.MESH,
        )

    own_slab = pltpu.make_async_copy(hid, X.at[0, 0], own.at[0])
    own_slab.start()
    own_head = [
        pltpu.make_async_copy(head.at[pl.ds(i * BLOCK, BLOCK)], H.at[0, i], own.at[1 + i])
        for i in range(2)
    ]
    for c in own_head:
        c.start()

    barrier = pltpu.get_barrier_semaphore()
    for d in (at_z(1), at_z(-1), at_x(1), at_x(-1)):
        pl.semaphore_signal(
            barrier, inc=1, device_id=(seg, d), device_id_type=pl.DeviceIdType.MESH
        )
    for rel in range(1, 8):
        pl.semaphore_signal(
            barrier,
            inc=1,
            device_id=(lax.rem(seg + rel, 8), v),
            device_id_type=pl.DeviceIdType.MESH,
        )
    tokens = lax.broadcasted_iota(jnp.int32, (TOK, TOK), 0)
    later = lax.broadcasted_iota(jnp.int32, (TOK, TOK), 1)
    upper = jnp.where(tokens < later, 1.0, 0.0).astype(BF16)
    blocks = lax.broadcasted_iota(jnp.int32, (128, TOK), 0)
    seen = jnp.zeros((128, 1), F32)
    codes = []
    for j in range(A):
        named = blocks == allowed[pl.ds(j, 1), :]
        hot = jnp.where(named, 1.0, 0.0)
        before = jnp.dot(hot.astype(BF16), upper, preferred_element_type=F32) + seen
        place = jnp.sum(jnp.where(named, before, 0.0), axis=0, keepdims=True)
        codes.append((allowed[pl.ds(j, 1), :] * CAP).astype(F32) + place)
        seen = seen + jnp.sum(hot, axis=1, keepdims=True)
    target = codes[0]
    for j in range(1, A):
        target = jnp.where(tslot[...] == j, codes[j], target)
    offset = toff[...].astype(F32)

    slot = lax.broadcasted_iota(jnp.int32, (CAP, TOK), 0)
    left, right, across = (lax.rem(x + s, NX) for s in (3, 1, 2))
    for i in range(2):
        for w in range(4):
            column = (x, (left, right)[i], (left, right)[i], across)[w]
            odd = (i, i, 1 - i, i)[w]
            which = (z * 8 + column * 2 + odd) * CAP
            rcode[i, pl.ds(w * CAP, CAP), :] = (slot + which).astype(F32)

    def hits(info, i, step):
        rows = rcode[i]
        if step is not None:
            rows = rows + ((lax.rem(z + step + NZ, NZ) - z) * 128).astype(F32)
        hit = rows == info[0:1, :]
        for j in range(1, A):
            hit = hit | (rows == info[j : j + 1, :])
        return hit

    def choose(hit):
        return jnp.where(hit, 1.0, 0.0).astype(BF16)

    named = jnp.concatenate(codes, axis=0)
    own_slab.wait()
    picks = []
    for d in range(2):
        step = 1 - 2 * d

        def marked(hit):
            return jnp.max(jnp.where(hit, 1.0, 0.0), axis=0, keepdims=True)

        last = marked(hits(named, d, 8))
        near = jnp.maximum(
            marked(hits(named, 0, 7 * step)), marked(hits(named, 1, 7 * step))
        )
        near = near * (1.0 - last)
        rest = 1.0 - last - near
        classes = jnp.concatenate([last, near, rest, jnp.zeros((13, TOK), F32)], axis=0)
        rank = jnp.dot(classes.astype(BF16), upper, preferred_element_type=F32)
        n_last = jnp.sum(last, axis=1, keepdims=True)
        n_near = jnp.sum(near, axis=1, keepdims=True)
        position = (
            last * rank[0:1]
            + near * (n_last + rank[1:2])
            + rest * (n_last + n_near + rank[2:3])
        )
        pick = jnp.where(tokens.astype(F32) == position, 1.0, 0.0)
        picks.append(pick)
        for c in range(2):
            rows = slice(c * 128, (c + 1) * 128)
            XS[d, rows] = jnp.dot(
                pick[rows].astype(BF16), X[0, 0], preferred_element_type=F32
            ).astype(BF16)
    for d in range(2):
        X[d, 7, 192:256] = jnp.zeros((64, SLAB), BF16)
        Z[d, 64:128] = jnp.zeros((64, SLAB), BF16)

    pl.semaphore_wait(barrier, 11)

    sides = (at_z(1), at_z(-1))

    def slab(k, d, c):
        begin, size = ((0, 64), (64, 64), (128, 64))[c] if k == 7 else (c * 128, 128)
        if k == 8:
            begin, size = 0, 64
        rows = pl.ds(begin, size)
        src = XS.at[d, rows] if k == 1 else X.at[d, k - 1, rows]
        dst = Z.at[d, rows] if k == 8 else X.at[d, k, rows]
        return push(src, dst, xs.at[d, k, c], xr.at[d, k, c], seg, sides[d])

    def meta(k, d):
        src = MS.at[d] if k == 1 else M.at[d, k - 1]
        return push(src, M.at[d, k], ms.at[d, k], mr.at[d, k], seg, sides[d])

    for c in range(2):
        for d in range(2):
            slab(1, d, c).start()

    first, second = head.at[pl.ds(0, BLOCK)], head.at[pl.ds(BLOCK, BLOCK)]

    def block(w, i):
        src = ((first, second), (second, first), (H.at[1, 0], H.at[1, 1]))[w - 1][i]
        return push(src, H.at[w, i], hs.at[w, i], hr.at[w, i], seg, at_x(1 - 2 * i))

    for i in range(2):
        block(1, i).start()

    squares = jnp.zeros((TOK, 128), F32)
    for c in range(SLAB // 128):
        part = X[0, 0, :, pl.ds(c * 128, 128)].astype(F32)
        squares = squares + part * part
    Sx[0] = jnp.sum(squares.T.reshape(16, 8, TOK), axis=0)

    def square(rel):
        return push(
            Sx.at[0], Sx.at[rel], ss.at[rel], sr.at[rel], lax.rem(seg + rel, 8), v
        )

    for rel in range(1, 8):
        square(rel).start()
    total = Sx[0]
    for rel in range(1, 8):
        square(rel).wait_recv()
        total = total + Sx[rel]
    scale = lax.rsqrt(jnp.sum(total, axis=0, keepdims=True) * (1.0 / D) + 1e-05)
    info = jnp.concatenate(codes + [scale, target, offset, offset], axis=0)
    M[0, 0] = info
    for d in range(2):
        MS[d] = lax.dot_general(
            info,
            picks[d],
            (((1,), (1,)), ((), ())),
            precision=lax.Precision.HIGHEST,
            preferred_element_type=F32,
        )
        meta(1, d).start()

    def keep(k, d, i, info, hit, picked):
        size = jnp.sum(jnp.where(hit, info[4:5, :], 0.0), axis=1, keepdims=True)
        normed = (picked * size * gain[...]).astype(BF16)
        for w in range(4):
            G[w, i, k, d] = normed[w * CAP : (w + 1) * CAP]

    def gather(k, d):
        info = M[d, k]
        for i in range(2):
            hit = hits(info, i, None)
            picked = jnp.dot(choose(hit), X[d, k], preferred_element_type=F32)
            keep(k, d, i, info, hit, picked)

    def gather_last():
        for i in range(2):
            info = M[i, 8]
            hit = hits(info, i, None)
            picked = jnp.dot(choose(hit)[:, 0:128], Z[i], preferred_element_type=F32)
            keep(0, 1, i, info, hit, picked)

    def spread(w, i, k0, count, logits):
        for d in range(2):
            for h in range(2):
                Pp[4 * i + 2 * h + d, pl.ds(k0, count), w] = logits[
                    :, d, :, 256 * h : 256 * (h + 1)
                ]

    def multiply(rows, w, i):
        return lax.dot_general(
            rows, H[w, i], (((1,), (1,)), ((), ())), preferred_element_type=F32
        )

    def products(w0, w1, k0, k1):
        count = k1 - k0

        def one(n, carry):
            w, i = n // 2, lax.rem(n, 2)
            rows = G[w, i, pl.ds(k0, count)].reshape(count * 2 * CAP, SLAB)
            logits = multiply(rows, w, i).reshape(count, 2, CAP, BLOCK).astype(BF16)
            spread(w, i, k0, count, logits)
            return carry

        lax.fori_loop(2 * w0, 2 * w1, one, 0)

    def products_flat(w0, w1, k):
        for w in range(w0, w1):
            for i in range(2):
                logits = multiply(G[w, i, k].reshape(2 * CAP, SLAB), w, i)
                spread(w, i, k, 1, logits.reshape(1, 2, CAP, BLOCK).astype(BF16))

    def products_last(w0, w1):
        for w in range(w0, w1):
            for i in range(2):
                logits = multiply(G[w, i, 0, 1], w, i).astype(BF16)
                for h in range(2):
                    Pp[4 * i + 2 * h + 1, 0, w] = logits[:, 256 * h : 256 * (h + 1)]

    def partial(r, rel):
        w0, w1, k0, k1, _ = ROUNDS[r]
        dest = lax.rem(seg + rel, 8)
        part = (pl.ds(k0, k1 - k0), pl.ds(w0, w1 - w0))
        return push(
            Pp.at[(dest, *part)],
            Pr.at[(rel, *part)],
            ps.at[r, rel],
            pr.at[r, rel],
            dest,
            v,
        )

    def each_peer(r, act):
        side = ROUNDS[r][4]

        def one(rel, carry):
            if side is None:
                act(partial(r, rel))
            else:

                @pl.when(lax.rem(seg + rel, 2) == side)
                def _():
                    act(partial(r, rel))

            return carry

        lax.fori_loop(1, 8, one, 0)

    def send(rounds):
        for r in rounds:
            each_peer(r, lambda copy: copy.start())

    def sent(rounds):
        for r in rounds:
            each_peer(r, lambda copy: copy.wait_send())

    def stats(rounds):
        for r in rounds:
            side = ROUNDS[r][4]
            if side is None:
                stats_of(r)
            else:
                pl.when(my_d == side)(functools.partial(stats_of, r))

    def stats_of(r):
        w0, w1, k0, k1, _ = ROUNDS[r]
        n = (w1 - w0) * CAP

        def arrive(rel, carry):
            partial(r, rel).wait_recv()
            return carry

        lax.fori_loop(1, 8, arrive, 0)

        last = r >= len(ROUNDS) - len(ROUND_E)

        def one(k, carry):
            span = pl.ds(w0, w1 - w0)
            logits = Pp[seg, k, span].reshape(n, 256).astype(F32)
            for rel in range(1, 8):
                logits = logits + Pr[rel, k, span].reshape(n, 256).astype(F32)
            info = M[my_i if last else my_d, 8 if last else k]
            rows = rcode[my_i, pl.ds(w0 * CAP, n), :]
            wanted = jnp.sum(
                jnp.where(rows == info[5:6, :], info[6:7, :] + 1.0, 0.0),
                axis=1,
                keepdims=True,
            )
            column = lax.broadcasted_iota(jnp.int32, (n, 256), 1) + 256 * my_h + 1
            peak = jnp.max(logits, axis=1, keepdims=True)
            mass = jnp.sum(jnp.exp(logits - peak), axis=1, keepdims=True)
            goal = jnp.sum(
                jnp.where(column.astype(F32) == wanted, logits, 0.0),
                axis=1,
                keepdims=True,
            )
            lane = lax.broadcasted_iota(jnp.int32, (n, 128), 1)
            St[k, pl.ds(w0 * CAP, n), :] = jnp.where(
                lane == 0, peak, jnp.where(lane == 1, mass, goal)
            )
            return carry

        if k1 - k0 == 1:
            one(k0, 0)
        else:
            lax.fori_loop(k0, k1, one, 0)

    def report(k):
        step = jnp.where(my_d == 0, -k, k)
        return push(Rs.at[k], Rr.at[k], ts.at[k], tr.at[k], seg, at_z(step))

    def turn(k):
        rows = St[k]
        Rs[k] = jnp.concatenate([rows, rows], axis=0).T[0:8]

    acc[...] = jnp.zeros((16, TOK), F32)

    def collect(k, step):
        plane = lax.rem(z + step + NZ, NZ) - z
        rows = rcode[my_i] + (plane * 128).astype(F32)
        columns = jnp.concatenate([Rr[k]] * 16, axis=0).T
        for j in range(A):
            match = rows == M[0, 0, j : j + 1, :]
            for q in range(3):
                acc[pl.ds(4 * q + j, 1), :] += jnp.sum(
                    jnp.where(match, columns[0:64, q : q + 1], 0.0), axis=0, keepdims=True
                )

    gather(0, 0)
    for w in range(4):
        for i in range(2):
            G[w, i, 0, 1] = jnp.zeros((CAP, SLAB), BF16)
    for c in own_head:
        c.wait()

    for n in range(3):
        shift = ((lax.rem(z + (7, 9, 8)[n], NZ) - z) * 128).astype(F32)
        for i in range(2):
            rows = rcode[i] + shift
            for j in range(A):
                table[n, i, :, pl.ds(j * TOK, TOK)] = jnp.where(
                    rows == named[j : j + 1], 1.0, 0.0
                )

    for k in range(1, 6):
        for d in range(2):
            slab(k, d, 0).wait_recv()
            slab(k + 1, d, 0).start()
        for d in range(2):
            slab(k, d, 1).wait_recv()
            meta(k, d).wait_recv()
            meta(k + 1, d).start()
            slab(k + 1, d, 1).start()
        for d in range(2):
            gather(k, d)
        if k == 2:
            for i in range(2):
                block(1, i).wait()
                block(2, i).start()
        if k == 3:
            products(0, 2, 0, 4)
            send((0, 1))
        if k == 4:
            for i in range(2):
                block(2, i).wait()
                block(3, i).start()
        if k == 5:
            products(0, 2, 4, 6)
            send((2,))
            products(2, 3, 0, 6)
            send((3, 4))
            stats((0, 1))

    for d in range(2):
        slab(6, d, 0).wait_recv()
        slab(7, d, 0).start()
        slab(7, d, 1).start()
    for d in range(2):
        slab(6, d, 1).wait_recv()
        meta(6, d).wait_recv()
        meta(7, d).start()
        slab(7, d, 2).start()
    for d in range(2):
        gather(6, d)
    products(0, 3, 6, 7)
    send((5,))
    for d in range(2):
        slab(7, d, 0).wait_recv()
        meta(7, d).wait_recv()
        meta(8, d).start()
        slab(8, d, 0).start()
    for i in range(2):
        block(3, i).wait()
    products(3, 4, 0, 7)
    send((6, 7))
    stats((2, 3, 4))

    for d in range(2):
        slab(7, d, 1).wait_recv()
        slab(7, d, 2).wait_recv()
    for d in range(2):
        gather(7, d)
    products_flat(0, 2, 7)
    send((8,))
    products_flat(2, 4, 7)
    send((9,))

    for d in range(2):
        slab(8, d, 0).wait_recv()
        meta(8, d).wait_recv()
    gather_last()
    products_last(0, 2)
    send((10,))
    products_last(2, 4)
    send((11,))

    stats((5, 6, 7))
    for k in range(1, 7):
        turn(k)
        report(k).start()

    @pl.when(my_d == 0)
    def _():
        turn(0)
        Rr[0] = Rs[0]

    def finish(n, rel):
        step = 8 if n == 2 else jnp.where(my_d == 0, -7, 7)
        place = n if n == 2 else my_d
        quarter = 2 * my_i + my_h
        return push(
            Qs.at[n // 2],
            Qr.at[place, quarter],
            qs.at[n // 2, rel],
            qr.at[place, quarter],
            lax.rem(seg + rel, 8),
            at_z(step),
        )

    def give(n, k):
        rows = St[k]
        turned = jnp.concatenate([rows, rows], axis=0).T
        lane = lax.broadcasted_iota(jnp.int32, (1, 128), 1)
        Qs[n // 2] = jnp.concatenate(
            [jnp.where(lane < 64, turned[0:1], turned[1:2]), turned[2:3]], axis=0
        )
        for rel in range(8):
            finish(n, rel).start()

    stats((8, 9))
    give(0, 7)
    stats((10, 11))

    @pl.when(my_d == 1)
    def _():
        give(2, 0)

    for k in range(1, 9):
        for d in range(2):
            for c in range(2 if k < 7 else (3, 1)[k - 7]):
                slab(k, d, c).wait_send()
            meta(k, d).wait_send()
    for rel in range(1, 8):
        square(rel).wait_send()
    sent(range(len(ROUNDS)))

    for k in range(1, 7):
        report(k).wait_recv()
        collect(k, jnp.where(my_d == 0, k, -k))

    @pl.when(my_d == 0)
    def _():
        collect(0, 0)

    peak, mass, goal = (acc[4 * q : 4 * q + 4] for q in range(3))
    have = mass > 0.5
    largest = jnp.max(jnp.where(have, peak, -1e30), axis=0, keepdims=True)
    weight = jnp.where(have, jnp.exp(jnp.where(have, peak - largest, 0.0)), 0.0)
    E[0] = jnp.concatenate(
        [
            largest,
            jnp.sum(mass * weight, axis=0, keepdims=True),
            jnp.sum(goal, axis=0, keepdims=True),
            jnp.zeros((5, TOK), F32),
        ],
        axis=0,
    )

    def share(rel):
        return push(E.at[0], E.at[rel], es.at[rel], er.at[rel], lax.rem(seg + rel, 8), v)

    for rel in range(1, 8):
        share(rel).start()
    for k in range(1, 7):
        report(k).wait_send()

    for rel in range(1, 8):
        share(rel).wait_recv()
    mine = []
    for n in range(3):
        for quarter in range(4):
            push(
                Qs.at[0], Qr.at[n, quarter], qs.at[0, 0], qr.at[n, quarter], seg, at_z(8)
            ).wait_recv()
        got = jnp.concatenate([Qr[n, quarter] for quarter in range(4)], axis=0)
        got = jnp.concatenate([got[:, 0:64], got[:, 64:128]], axis=0)
        for i in range(2):
            found = jnp.dot(
                got,
                table[n, i],
                precision=lax.Precision.HIGHEST,
                preferred_element_type=F32,
            )
            for h in range(2):
                row = 4 * i + 2 * h
                mine.append(
                    (found[row : row + 1], found[row + 8 : row + 9], found[row + 1 : row + 2])
                )
    peak, mass, goal = (jnp.concatenate(rows, axis=0) for rows in zip(*mine))
    here = mass > 0.5
    marked_peak = jnp.where(here, peak, -1e30)
    best = jnp.max(marked_peak, axis=0, keepdims=True)
    top_here = functools.reduce(
        jnp.maximum, [best[:, j * TOK : (j + 1) * TOK] for j in range(A)]
    )
    top = E[0, 0:1]
    for rel in range(1, 8):
        top = jnp.maximum(top, E[rel, 0:1])
    top = jnp.maximum(top, top_here)
    weight = jnp.exp(marked_peak - jnp.concatenate([top] * A, axis=1))
    mass_here = jnp.sum(jnp.where(here, mass * weight, 0.0), axis=0, keepdims=True)
    goal_here = jnp.sum(goal, axis=0, keepdims=True)
    mass = sum(mass_here[:, j * TOK : (j + 1) * TOK] for j in range(A))
    goal = sum(goal_here[:, j * TOK : (j + 1) * TOK] for j in range(A))
    for rel in range(8):
        mass = mass + E[rel, 1:2] * jnp.exp(E[rel, 0:1] - top)
        goal = goal + E[rel, 2:3]
    out[...] = goal - (top + jnp.log(mass))
    for rel in range(1, 8):
        share(rel).wait_send()

    for rel in range(8):
        finish(0, rel).wait_send()

    @pl.when(my_d == 1)
    def _():
        for rel in range(8):
            finish(2, rel).wait_send()


def per_device(hidden, norm_gain, head, allowed, target_slot, target_offset):
    vmem = pl.BlockSpec(memory_space=pltpu.VMEM)
    hbm = pl.BlockSpec(memory_space=pl.ANY)
    dma = pltpu.SemaphoreType.DMA
    out = pl.pallas_call(
        kernel,
        out_shape=jax.ShapeDtypeStruct((1, TOK), F32),
        in_specs=[hbm, vmem, hbm, vmem, vmem, vmem],
        out_specs=vmem,
        scratch_shapes=[
            pltpu.VMEM((2, 8, TOK, SLAB), BF16),
            pltpu.VMEM((2, TOK, SLAB), BF16),
            pltpu.VMEM((2, 128, SLAB), BF16),
            pltpu.VMEM((2, 9, 8, TOK), F32),
            pltpu.VMEM((2, 8, TOK), F32),
            pltpu.VMEM((4, 2, BLOCK, SLAB), BF16),
            pltpu.VMEM((4, 2, 8, 2, CAP, SLAB), BF16),
            pltpu.VMEM((8, 8, 4, CAP, 256), BF16),
            pltpu.VMEM((8, 8, 4, CAP, 256), BF16),
            pltpu.VMEM((8, 64, 128), F32),
            pltpu.VMEM((8, 8, 128), F32),
            pltpu.VMEM((8, 8, 128), F32),
            pltpu.VMEM((2, 2, 128), F32),
            pltpu.VMEM((3, 4, 2, 128), F32),
            pltpu.VMEM((3, 2, 64, A * TOK), F32),
            pltpu.VMEM((2, 64, TOK), F32),
            pltpu.VMEM((8, 8, TOK), F32),
            pltpu.VMEM((8, 8, TOK), F32),
            pltpu.VMEM((16, TOK), F32),
            dma((2, 9, 3)),
            dma((2, 9, 3)),
            dma((2, 9)),
            dma((2, 9)),
            dma((4, 2)),
            dma((4, 2)),
            dma((len(ROUNDS), 8)),
            dma((len(ROUNDS), 8)),
            dma((8,)),
            dma((8,)),
            dma((8,)),
            dma((8,)),
            dma((8,)),
            dma((8,)),
            dma((2, 8)),
            dma((3, 4)),
            dma((3,)),
        ],
        compiler_params=pltpu.CompilerParams(
            collective_id=0, has_side_effects=True, vmem_limit_bytes=56 * 2**20
        ),
    )(
        hidden,
        norm_gain.reshape(1, SLAB),
        head,
        allowed,
        target_slot.reshape(1, TOK),
        target_offset.reshape(1, TOK),
    )
    return out.reshape(TOK)


def solution(mesh):
    return jax.shard_map(
        per_device,
        mesh=mesh,
        in_specs=(
            P("vocab", "segment"),
            P("segment"),
            P("vocab", "segment"),
            P(None, "vocab"),
            P("vocab"),
            P("vocab"),
        ),
        out_specs=P("vocab"),
        check_vma=False,
    )
```

```python
import functools

import jax
import jax.numpy as jnp
from jax import lax
from jax.experimental import pallas as pl
from jax.experimental.pallas import tpu as pltpu
from jax.sharding import PartitionSpec as P

D = 8192
BLOCK = 512
A = 4
CAP = 16
NZ = 16
NX = 4
TOK = 256
SLAB = 1024
F32 = jnp.float32
BF16 = jnp.bfloat16
ROUND_A = ((0, 2, 1, 4, None), (0, 2, 0, 1, 0))
ROUND_B = ((0, 2, 4, 6, None), (2, 3, 1, 6, None), (2, 3, 0, 1, 0))
ROUND_C = ((0, 3, 6, 7, None), (3, 4, 1, 7, None), (3, 4, 0, 1, 0))
ROUND_D = ((0, 2, 7, 8, None), (2, 4, 7, 8, None))
ROUND_E = ((0, 2, 0, 1, 1), (2, 4, 0, 1, 1))
ROUNDS = ROUND_A + ROUND_B + ROUND_C + ROUND_D + ROUND_E
PAIRED = 6


def kernel(
    hid,
    gain,
    head,
    allowed,
    tslot,
    toff,
    out,
    X,
    XS,
    Z,
    M,
    MS,
    H,
    G,
    Pp,
    Pr,
    St,
    Rs,
    Rr,
    Qs,
    Qr,
    table,
    Lm,
    Ls,
    Lr,
    rcode,
    Sx,
    E,
    acc,
    xs,
    xr,
    ms,
    mr,
    hs,
    hr,
    ps,
    pr,
    ss,
    sr,
    es,
    er,
    ts,
    tr,
    qs,
    qr,
    own,
):
    seg = lax.axis_index("segment")
    v = lax.axis_index("vocab")
    z = v // NX
    x = lax.rem(v, NX)
    my_i = seg // 4
    my_h = lax.rem(seg // 2, 2)
    my_d = lax.rem(seg, 2)

    def at_z(step):
        return lax.rem(z + step + NZ, NZ) * NX + x

    def at_x(step):
        return z * NX + lax.rem(x + step + NX, NX)

    def push(src, dst, send, recv, s, d):
        return pltpu.make_async_remote_copy(
            src_ref=src,
            dst_ref=dst,
            send_sem=send,
            recv_sem=recv,
            device_id=(s, d),
            device_id_type=pl.DeviceIdType.MESH,
        )

    own_slab = pltpu.make_async_copy(hid, X.at[0, 0], own.at[0])
    own_slab.start()
    own_head = [
        pltpu.make_async_copy(head.at[pl.ds(i * BLOCK, BLOCK)], H.at[0, i], own.at[1 + i])
        for i in range(2)
    ]
    for c in own_head:
        c.start()

    barrier = pltpu.get_barrier_semaphore()
    for d in (at_z(1), at_z(-1), at_x(1), at_x(-1)):
        pl.semaphore_signal(
            barrier, inc=1, device_id=(seg, d), device_id_type=pl.DeviceIdType.MESH
        )
    for rel in range(1, 8):
        pl.semaphore_signal(
            barrier,
            inc=1,
            device_id=(lax.rem(seg + rel, 8), v),
            device_id_type=pl.DeviceIdType.MESH,
        )
    tokens = lax.broadcasted_iota(jnp.int32, (TOK, TOK), 0)
    later = lax.broadcasted_iota(jnp.int32, (TOK, TOK), 1)
    upper = jnp.where(tokens < later, 1.0, 0.0).astype(BF16)
    blocks = lax.broadcasted_iota(jnp.int32, (128, TOK), 0)
    seen = jnp.zeros((128, 1), F32)
    codes = []
    for j in range(A):
        named = blocks == allowed[pl.ds(j, 1), :]
        hot = jnp.where(named, 1.0, 0.0)
        before = jnp.dot(hot.astype(BF16), upper, preferred_element_type=F32) + seen
        place = jnp.sum(jnp.where(named, before, 0.0), axis=0, keepdims=True)
        codes.append((allowed[pl.ds(j, 1), :] * CAP).astype(F32) + place)
        seen = seen + jnp.sum(hot, axis=1, keepdims=True)
    target = codes[0]
    for j in range(1, A):
        target = jnp.where(tslot[...] == j, codes[j], target)
    offset = toff[...].astype(F32)

    slot = lax.broadcasted_iota(jnp.int32, (CAP, TOK), 0)
    left, right, across = (lax.rem(x + s, NX) for s in (3, 1, 2))
    for i in range(2):
        for w in range(4):
            column = (x, (left, right)[i], (left, right)[i], across)[w]
            odd = (i, i, 1 - i, i)[w]
            which = (z * 8 + column * 2 + odd) * CAP
            rcode[i, pl.ds(w * CAP, CAP), :] = (slot + which).astype(F32)

    def hits(info, i, step):
        rows = rcode[i]
        if step is not None:
            rows = rows + ((lax.rem(z + step + NZ, NZ) - z) * 128).astype(F32)
        hit = rows == info[0:1, :]
        for j in range(1, A):
            hit = hit | (rows == info[j : j + 1, :])
        return hit

    def choose(hit):
        return jnp.where(hit, 1.0, 0.0).astype(BF16)

    named = jnp.concatenate(codes, axis=0)
    own_slab.wait()
    picks = []
    for d in range(2):
        step = 1 - 2 * d

        def marked(hit):
            return jnp.max(jnp.where(hit, 1.0, 0.0), axis=0, keepdims=True)

        last = marked(hits(named, d, 8))
        near = jnp.maximum(
            marked(hits(named, 0, 7 * step)), marked(hits(named, 1, 7 * step))
        )
        near = near * (1.0 - last)
        rest = 1.0 - last - near
        classes = jnp.concatenate([last, near, rest, jnp.zeros((13, TOK), F32)], axis=0)
        rank = jnp.dot(classes.astype(BF16), upper, preferred_element_type=F32)
        n_last = jnp.sum(last, axis=1, keepdims=True)
        n_near = jnp.sum(near, axis=1, keepdims=True)
        position = (
            last * rank[0:1]
            + near * (n_last + rank[1:2])
            + rest * (n_last + n_near + rank[2:3])
        )
        pick = jnp.where(tokens.astype(F32) == position, 1.0, 0.0)
        picks.append(pick)
        for c in range(2):
            rows = slice(c * 128, (c + 1) * 128)
            XS[d, rows] = jnp.dot(
                pick[rows].astype(BF16), X[0, 0], preferred_element_type=F32
            ).astype(BF16)
    for d in range(2):
        X[d, 7, 192:256] = jnp.zeros((64, SLAB), BF16)
        Z[d, 64:128] = jnp.zeros((64, SLAB), BF16)

    pl.semaphore_wait(barrier, 11)

    sides = (at_z(1), at_z(-1))

    def slab(k, d, c):
        begin, size = ((0, 64), (64, 64), (128, 64))[c] if k == 7 else (c * 128, 128)
        if k == 8:
            begin, size = 0, 64
        rows = pl.ds(begin, size)
        src = XS.at[d, rows] if k == 1 else X.at[d, k - 1, rows]
        dst = Z.at[d, rows] if k == 8 else X.at[d, k, rows]
        return push(src, dst, xs.at[d, k, c], xr.at[d, k, c], seg, sides[d])

    def meta(k, d):
        src = MS.at[d] if k == 1 else M.at[d, k - 1]
        return push(src, M.at[d, k], ms.at[d, k], mr.at[d, k], seg, sides[d])

    for c in range(2):
        for d in range(2):
            slab(1, d, c).start()

    first, second = head.at[pl.ds(0, BLOCK)], head.at[pl.ds(BLOCK, BLOCK)]

    def block(w, i):
        src = ((first, second), (second, first), (H.at[1, 0], H.at[1, 1]))[w - 1][i]
        return push(src, H.at[w, i], hs.at[w, i], hr.at[w, i], seg, at_x(1 - 2 * i))

    for i in range(2):
        block(1, i).start()

    squares = jnp.zeros((TOK, 128), F32)
    for c in range(SLAB // 128):
        part = X[0, 0, :, pl.ds(c * 128, 128)].astype(F32)
        squares = squares + part * part
    Sx[0] = jnp.sum(squares.T.reshape(16, 8, TOK), axis=0)

    def square(rel):
        return push(
            Sx.at[0], Sx.at[rel], ss.at[rel], sr.at[rel], lax.rem(seg + rel, 8), v
        )

    for rel in range(1, 8):
        square(rel).start()
    total = Sx[0]
    for rel in range(1, 8):
        square(rel).wait_recv()
        total = total + Sx[rel]
    scale = lax.rsqrt(jnp.sum(total, axis=0, keepdims=True) * (1.0 / D) + 1e-05)
    info = jnp.concatenate(codes + [scale, target, offset, offset], axis=0)
    M[0, 0] = info
    for d in range(2):
        MS[d] = lax.dot_general(
            info,
            picks[d],
            (((1,), (1,)), ((), ())),
            precision=lax.Precision.HIGHEST,
            preferred_element_type=F32,
        )
        meta(1, d).start()

    def keep(k, d, i, info, hit, picked):
        size = jnp.sum(jnp.where(hit, info[4:5, :], 0.0), axis=1, keepdims=True)
        normed = (picked * size * gain[...]).astype(BF16)
        for w in range(4):
            G[w, i, k, d] = normed[w * CAP : (w + 1) * CAP]

    def gather(k, d):
        info = M[d, k]
        for i in range(2):
            hit = hits(info, i, None)
            picked = jnp.dot(choose(hit), X[d, k], preferred_element_type=F32)
            keep(k, d, i, info, hit, picked)

    def gather_last():
        for i in range(2):
            info = M[i, 8]
            hit = hits(info, i, None)
            picked = jnp.dot(choose(hit)[:, 0:128], Z[i], preferred_element_type=F32)
            keep(0, 1, i, info, hit, picked)

    def spread(w, i, k0, count, logits):
        for d in range(2):
            for h in range(2):
                Pp[4 * i + 2 * h + d, pl.ds(k0, count), w] = logits[
                    :, d, :, 256 * h : 256 * (h + 1)
                ]

    def multiply(rows, w, i):
        return lax.dot_general(
            rows, H[w, i], (((1,), (1,)), ((), ())), preferred_element_type=F32
        )

    def products(w0, w1, k0, k1):
        count = k1 - k0

        def one(n, carry):
            w, i = n // 2, lax.rem(n, 2)
            rows = G[w, i, pl.ds(k0, count)].reshape(count * 2 * CAP, SLAB)
            logits = multiply(rows, w, i).reshape(count, 2, CAP, BLOCK).astype(BF16)
            spread(w, i, k0, count, logits)
            return carry

        lax.fori_loop(2 * w0, 2 * w1, one, 0)

    def products_flat(w0, w1, k):
        for w in range(w0, w1):
            for i in range(2):
                logits = multiply(G[w, i, k].reshape(2 * CAP, SLAB), w, i)
                spread(w, i, k, 1, logits.reshape(1, 2, CAP, BLOCK).astype(BF16))

    def products_last(w0, w1):
        for w in range(w0, w1):
            for i in range(2):
                logits = multiply(G[w, i, 0, 1], w, i).astype(BF16)
                for h in range(2):
                    Pp[4 * i + 2 * h + 1, 0, w] = logits[:, 256 * h : 256 * (h + 1)]

    def products_pair():
        for i in range(2):
            rows = G[3, i, pl.ds(0, 7)].reshape(7 * 2 * CAP, SLAB)
            logits = multiply(rows, 3, i).reshape(7, 2, CAP, BLOCK)
            mine = jnp.where(my_d == 0, logits[1:7, 0], logits[1:7, 1])
            others = jnp.where(my_d == 0, logits[1:7, 1], logits[1:7, 0])
            for h in range(2):
                span = slice(256 * h, 256 * (h + 1))
                Lm[2 * i + h] = mine[:, :, span]
                Ls[2 * i + h] = others[:, :, span]
                Pp[4 * i + 2 * h, 0, 3] = logits[0, 0, :, span].astype(BF16)

    def pair():
        return push(Ls, Lr, own.at[3], own.at[4], seg + 1 - 2 * my_d, v)

    def add_pair():
        for n in range(4):
            Pp[2 * n + my_d, 1:7, 3] = (Lm[n] + Lr[n]).astype(BF16)

    def partial(r, rel):
        w0, w1, k0, k1, _ = ROUNDS[r]
        dest = lax.rem(seg + rel, 8)
        part = (pl.ds(k0, k1 - k0), pl.ds(w0, w1 - w0))
        return push(
            Pp.at[(dest, *part)],
            Pr.at[(rel, *part)],
            ps.at[r, rel],
            pr.at[r, rel],
            dest,
            v,
        )

    def each_peer(r, act):
        side = ROUNDS[r][4]

        if r == PAIRED:
            for rel in (2, 4, 6):
                act(partial(r, rel))
            return

        def one(rel, carry):
            if side is None:
                act(partial(r, rel))
            else:

                @pl.when(lax.rem(seg + rel, 2) == side)
                def _():
                    act(partial(r, rel))

            return carry

        lax.fori_loop(1, 8, one, 0)

    def send(rounds):
        for r in rounds:
            each_peer(r, lambda copy: copy.start())

    def sent(rounds):
        for r in rounds:
            each_peer(r, lambda copy: copy.wait_send())

    def stats(rounds):
        for r in rounds:
            side = ROUNDS[r][4]
            if side is None:
                stats_of(r)
            else:
                pl.when(my_d == side)(functools.partial(stats_of, r))

    def stats_of(r):
        w0, w1, k0, k1, _ = ROUNDS[r]
        n = (w1 - w0) * CAP

        def arrive(rel, carry):
            partial(r, rel).wait_recv()
            return carry

        if r == PAIRED:
            for rel in (2, 4, 6):
                partial(r, rel).wait_recv()
        else:
            lax.fori_loop(1, 8, arrive, 0)

        last = r >= len(ROUNDS) - len(ROUND_E)

        def one(k, carry):
            span = pl.ds(w0, w1 - w0)
            logits = Pp[seg, k, span].reshape(n, 256).astype(F32)
            for rel in (2, 4, 6) if r == PAIRED else range(1, 8):
                logits = logits + Pr[rel, k, span].reshape(n, 256).astype(F32)
            info = M[my_i if last else my_d, 8 if last else k]
            rows = rcode[my_i, pl.ds(w0 * CAP, n), :]
            wanted = jnp.sum(
                jnp.where(rows == info[5:6, :], info[6:7, :] + 1.0, 0.0),
                axis=1,
                keepdims=True,
            )
            column = lax.broadcasted_iota(jnp.int32, (n, 256), 1) + 256 * my_h + 1
            peak = jnp.max(logits, axis=1, keepdims=True)
            mass = jnp.sum(jnp.exp(logits - peak), axis=1, keepdims=True)
            goal = jnp.sum(
                jnp.where(column.astype(F32) == wanted, logits, 0.0),
                axis=1,
                keepdims=True,
            )
            lane = lax.broadcasted_iota(jnp.int32, (n, 128), 1)
            St[k, pl.ds(w0 * CAP, n), :] = jnp.where(
                lane == 0, peak, jnp.where(lane == 1, mass, goal)
            )
            return carry

        if k1 - k0 == 1:
            one(k0, 0)
        else:
            lax.fori_loop(k0, k1, one, 0)

    def report(k):
        step = jnp.where(my_d == 0, -k, k)
        return push(Rs.at[k], Rr.at[k], ts.at[k], tr.at[k], seg, at_z(step))

    def turn(k):
        rows = St[k]
        Rs[k] = jnp.concatenate([rows, rows], axis=0).T[0:8]

    acc[...] = jnp.zeros((16, TOK), F32)

    def collect(k, step):
        plane = lax.rem(z + step + NZ, NZ) - z
        rows = rcode[my_i] + (plane * 128).astype(F32)
        columns = jnp.concatenate([Rr[k]] * 16, axis=0).T
        for j in range(A):
            match = rows == M[0, 0, j : j + 1, :]
            for q in range(3):
                acc[pl.ds(4 * q + j, 1), :] += jnp.sum(
                    jnp.where(match, columns[0:64, q : q + 1], 0.0), axis=0, keepdims=True
                )

    gather(0, 0)
    for w in range(4):
        for i in range(2):
            G[w, i, 0, 1] = jnp.zeros((CAP, SLAB), BF16)
    for c in own_head:
        c.wait()

    for n in range(3):
        shift = ((lax.rem(z + (7, 9, 8)[n], NZ) - z) * 128).astype(F32)
        for i in range(2):
            rows = rcode[i] + shift
            for j in range(A):
                table[n, i, :, pl.ds(j * TOK, TOK)] = jnp.where(
                    rows == named[j : j + 1], 1.0, 0.0
                )

    for k in range(1, 6):
        for d in range(2):
            slab(k, d, 0).wait_recv()
            slab(k + 1, d, 0).start()
        for d in range(2):
            slab(k, d, 1).wait_recv()
            meta(k, d).wait_recv()
            meta(k + 1, d).start()
            slab(k + 1, d, 1).start()
        for d in range(2):
            gather(k, d)
        if k == 1:
            for i in range(2):
                block(2, i).start()
        if k == 3:
            for i in range(2):
                block(1, i).wait()
                block(3, i).start()
            products(0, 2, 0, 4)
            send((0, 1))
        if k == 5:
            products(0, 2, 4, 6)
            send((2,))
            for i in range(2):
                block(2, i).wait()
            products(2, 3, 0, 6)
            send((3, 4))
            stats((0, 1))

    for d in range(2):
        slab(6, d, 0).wait_recv()
        slab(7, d, 0).start()
        slab(7, d, 1).start()
    for d in range(2):
        slab(6, d, 1).wait_recv()
        meta(6, d).wait_recv()
        meta(7, d).start()
        slab(7, d, 2).start()
    for d in range(2):
        gather(6, d)
    products(0, 3, 6, 7)
    send((5,))
    for d in range(2):
        slab(7, d, 0).wait_recv()
        meta(7, d).wait_recv()
        meta(8, d).start()
        slab(8, d, 0).start()
    for i in range(2):
        block(3, i).wait()
    products_pair()
    pair().start()
    send((7,))
    stats((2, 3, 4))
    pair().wait()
    add_pair()
    send((PAIRED,))

    for d in range(2):
        slab(7, d, 1).wait_recv()
        slab(7, d, 2).wait_recv()
    for d in range(2):
        gather(7, d)
    products_flat(0, 2, 7)
    send((8,))
    products_flat(2, 4, 7)
    send((9,))

    for d in range(2):
        slab(8, d, 0).wait_recv()
        meta(8, d).wait_recv()
    gather_last()
    products_last(0, 2)
    send((10,))
    products_last(2, 4)
    send((11,))

    stats((5, 6, 7))
    for k in range(1, 7):
        turn(k)
        report(k).start()

    @pl.when(my_d == 0)
    def _():
        turn(0)
        Rr[0] = Rs[0]

    def finish(n, rel):
        step = 8 if n == 2 else jnp.where(my_d == 0, -7, 7)
        place = n if n == 2 else my_d
        quarter = 2 * my_i + my_h
        return push(
            Qs.at[n // 2],
            Qr.at[place, quarter],
            qs.at[n // 2, rel],
            qr.at[place, quarter],
            lax.rem(seg + rel, 8),
            at_z(step),
        )

    def give(n, k):
        rows = St[k]
        turned = jnp.concatenate([rows, rows], axis=0).T
        lane = lax.broadcasted_iota(jnp.int32, (1, 128), 1)
        Qs[n // 2] = jnp.concatenate(
            [jnp.where(lane < 64, turned[0:1], turned[1:2]), turned[2:3]], axis=0
        )
        for rel in range(8):
            finish(n, rel).start()

    stats((8, 9))
    give(0, 7)
    stats((10, 11))

    @pl.when(my_d == 1)
    def _():
        give(2, 0)

    for k in range(1, 9):
        for d in range(2):
            for c in range(2 if k < 7 else (3, 1)[k - 7]):
                slab(k, d, c).wait_send()
            meta(k, d).wait_send()
    for rel in range(1, 8):
        square(rel).wait_send()
    sent(range(len(ROUNDS)))

    for k in range(1, 7):
        report(k).wait_recv()
        collect(k, jnp.where(my_d == 0, k, -k))

    @pl.when(my_d == 0)
    def _():
        collect(0, 0)

    peak, mass, goal = (acc[4 * q : 4 * q + 4] for q in range(3))
    have = mass > 0.5
    largest = jnp.max(jnp.where(have, peak, -1e30), axis=0, keepdims=True)
    weight = jnp.where(have, jnp.exp(jnp.where(have, peak - largest, 0.0)), 0.0)
    E[0] = jnp.concatenate(
        [
            largest,
            jnp.sum(mass * weight, axis=0, keepdims=True),
            jnp.sum(goal, axis=0, keepdims=True),
            jnp.zeros((5, TOK), F32),
        ],
        axis=0,
    )

    def share(rel):
        return push(E.at[0], E.at[rel], es.at[rel], er.at[rel], lax.rem(seg + rel, 8), v)

    for rel in range(1, 8):
        share(rel).start()
    for k in range(1, 7):
        report(k).wait_send()

    for rel in range(1, 8):
        share(rel).wait_recv()
    mine = []
    for n in range(3):
        for quarter in range(4):
            push(
                Qs.at[0], Qr.at[n, quarter], qs.at[0, 0], qr.at[n, quarter], seg, at_z(8)
            ).wait_recv()
        got = jnp.concatenate([Qr[n, quarter] for quarter in range(4)], axis=0)
        got = jnp.concatenate([got[:, 0:64], got[:, 64:128]], axis=0)
        for i in range(2):
            found = jnp.dot(
                got,
                table[n, i],
                precision=lax.Precision.HIGHEST,
                preferred_element_type=F32,
            )
            for h in range(2):
                row = 4 * i + 2 * h
                mine.append(
                    (found[row : row + 1], found[row + 8 : row + 9], found[row + 1 : row + 2])
                )
    peak, mass, goal = (jnp.concatenate(rows, axis=0) for rows in zip(*mine))
    here = mass > 0.5
    marked_peak = jnp.where(here, peak, -1e30)
    best = jnp.max(marked_peak, axis=0, keepdims=True)
    top_here = functools.reduce(
        jnp.maximum, [best[:, j * TOK : (j + 1) * TOK] for j in range(A)]
    )
    top = E[0, 0:1]
    for rel in range(1, 8):
        top = jnp.maximum(top, E[rel, 0:1])
    top = jnp.maximum(top, top_here)
    weight = jnp.exp(marked_peak - jnp.concatenate([top] * A, axis=1))
    mass_here = jnp.sum(jnp.where(here, mass * weight, 0.0), axis=0, keepdims=True)
    goal_here = jnp.sum(goal, axis=0, keepdims=True)
    mass = sum(mass_here[:, j * TOK : (j + 1) * TOK] for j in range(A))
    goal = sum(goal_here[:, j * TOK : (j + 1) * TOK] for j in range(A))
    for rel in range(8):
        mass = mass + E[rel, 1:2] * jnp.exp(E[rel, 0:1] - top)
        goal = goal + E[rel, 2:3]
    out[...] = goal - (top + jnp.log(mass))
    for rel in range(1, 8):
        share(rel).wait_send()

    for rel in range(8):
        finish(0, rel).wait_send()

    @pl.when(my_d == 1)
    def _():
        for rel in range(8):
            finish(2, rel).wait_send()


def per_device(hidden, norm_gain, head, allowed, target_slot, target_offset):
    vmem = pl.BlockSpec(memory_space=pltpu.VMEM)
    hbm = pl.BlockSpec(memory_space=pl.ANY)
    dma = pltpu.SemaphoreType.DMA
    out = pl.pallas_call(
        kernel,
        out_shape=jax.ShapeDtypeStruct((1, TOK), F32),
        in_specs=[hbm, vmem, hbm, vmem, vmem, vmem],
        out_specs=vmem,
        scratch_shapes=[
            pltpu.VMEM((2, 8, TOK, SLAB), BF16),
            pltpu.VMEM((2, TOK, SLAB), BF16),
            pltpu.VMEM((2, 128, SLAB), BF16),
            pltpu.VMEM((2, 9, 8, TOK), F32),
            pltpu.VMEM((2, 8, TOK), F32),
            pltpu.VMEM((4, 2, BLOCK, SLAB), BF16),
            pltpu.VMEM((4, 2, 8, 2, CAP, SLAB), BF16),
            pltpu.VMEM((8, 8, 4, CAP, 256), BF16),
            pltpu.VMEM((8, 8, 4, CAP, 256), BF16),
            pltpu.VMEM((8, 64, 128), F32),
            pltpu.VMEM((8, 8, 128), F32),
            pltpu.VMEM((8, 8, 128), F32),
            pltpu.VMEM((2, 2, 128), F32),
            pltpu.VMEM((3, 4, 2, 128), F32),
            pltpu.VMEM((3, 2, 64, A * TOK), F32),
            pltpu.VMEM((4, 6, CAP, 256), F32),
            pltpu.VMEM((4, 6, CAP, 256), F32),
            pltpu.VMEM((4, 6, CAP, 256), F32),
            pltpu.VMEM((2, 64, TOK), F32),
            pltpu.VMEM((8, 8, TOK), F32),
            pltpu.VMEM((8, 8, TOK), F32),
            pltpu.VMEM((16, TOK), F32),
            dma((2, 9, 3)),
            dma((2, 9, 3)),
            dma((2, 9)),
            dma((2, 9)),
            dma((4, 2)),
            dma((4, 2)),
            dma((len(ROUNDS), 8)),
            dma((len(ROUNDS), 8)),
            dma((8,)),
            dma((8,)),
            dma((8,)),
            dma((8,)),
            dma((8,)),
            dma((8,)),
            dma((2, 8)),
            dma((3, 4)),
            dma((5,)),
        ],
        compiler_params=pltpu.CompilerParams(
            collective_id=0, has_side_effects=True, vmem_limit_bytes=56 * 2**20
        ),
    )(
        hidden,
        norm_gain.reshape(1, SLAB),
        head,
        allowed,
        target_slot.reshape(1, TOK),
        target_offset.reshape(1, TOK),
    )
    return out.reshape(TOK)


def solution(mesh):
    return jax.shard_map(
        per_device,
        mesh=mesh,
        in_specs=(
            P("vocab", "segment"),
            P("segment"),
            P("vocab", "segment"),
            P(None, "vocab"),
            P("vocab"),
            P("vocab"),
        ),
        out_specs=P("vocab"),
        check_vma=False,
    )
```

```python
import functools

import jax
import jax.numpy as jnp
from jax import lax
from jax.experimental import pallas as pl
from jax.experimental.pallas import tpu as pltpu
from jax.sharding import PartitionSpec as P

D = 8192
BLOCK = 512
A = 4
CAP = 16
NZ = 16
NX = 4
TOK = 256
SLAB = 1024
F32 = jnp.float32
BF16 = jnp.bfloat16
ROUND_A = ((0, 2, 1, 4, None), (0, 2, 0, 1, 0))
ROUND_B = ((0, 2, 4, 6, None), (2, 3, 1, 6, None), (2, 3, 0, 1, 0))
ROUND_C = ((0, 3, 6, 7, None), (3, 4, 1, 7, None), (3, 4, 0, 1, 0))
ROUND_D = ((0, 2, 7, 8, None), (2, 4, 7, 8, None))
ROUND_E = ((0, 2, 0, 1, 1), (2, 4, 0, 1, 1))
ROUNDS = ROUND_A + ROUND_B + ROUND_C + ROUND_D + ROUND_E
PAIRED = 6


def kernel(
    hid,
    gain,
    head,
    allowed,
    tslot,
    toff,
    out,
    X,
    XS,
    Z,
    M,
    MS,
    H,
    G,
    Pp,
    Pr,
    St,
    Rs,
    Rr,
    Qs,
    Qr,
    table,
    Lm,
    Ls,
    Lr,
    rcode,
    Sx,
    E,
    acc,
    xs,
    xr,
    ms,
    mr,
    hs,
    hr,
    ps,
    pr,
    ss,
    sr,
    es,
    er,
    ts,
    tr,
    qs,
    qr,
    own,
):
    seg = lax.axis_index("segment")
    v = lax.axis_index("vocab")
    z = v // NX
    x = lax.rem(v, NX)
    my_i = seg // 4
    my_h = lax.rem(seg // 2, 2)
    my_d = lax.rem(seg, 2)

    def at_z(step):
        return lax.rem(z + step + NZ, NZ) * NX + x

    def at_x(step):
        return z * NX + lax.rem(x + step + NX, NX)

    def push(src, dst, send, recv, s, d):
        return pltpu.make_async_remote_copy(
            src_ref=src,
            dst_ref=dst,
            send_sem=send,
            recv_sem=recv,
            device_id=(s, d),
            device_id_type=pl.DeviceIdType.MESH,
        )

    own_slab = pltpu.make_async_copy(hid, X.at[0, 0], own.at[0])
    own_slab.start()
    own_head = [
        pltpu.make_async_copy(head.at[pl.ds(i * BLOCK, BLOCK)], H.at[0, i], own.at[1 + i])
        for i in range(2)
    ]
    for c in own_head:
        c.start()

    barrier = pltpu.get_barrier_semaphore()
    for d in (at_z(1), at_z(-1), at_x(1), at_x(-1)):
        pl.semaphore_signal(
            barrier, inc=1, device_id=(seg, d), device_id_type=pl.DeviceIdType.MESH
        )
    for rel in range(1, 8):
        pl.semaphore_signal(
            barrier,
            inc=1,
            device_id=(lax.rem(seg + rel, 8), v),
            device_id_type=pl.DeviceIdType.MESH,
        )
    tokens = lax.broadcasted_iota(jnp.int32, (TOK, TOK), 0)
    later = lax.broadcasted_iota(jnp.int32, (TOK, TOK), 1)
    upper = jnp.where(tokens < later, 1.0, 0.0).astype(BF16)
    blocks = lax.broadcasted_iota(jnp.int32, (128, TOK), 0)
    seen = jnp.zeros((128, 1), F32)
    codes = []
    for j in range(A):
        named = blocks == allowed[pl.ds(j, 1), :]
        hot = jnp.where(named, 1.0, 0.0)
        before = jnp.dot(hot.astype(BF16), upper, preferred_element_type=F32) + seen
        place = jnp.sum(jnp.where(named, before, 0.0), axis=0, keepdims=True)
        codes.append((allowed[pl.ds(j, 1), :] * CAP).astype(F32) + place)
        seen = seen + jnp.sum(hot, axis=1, keepdims=True)
    target = codes[0]
    for j in range(1, A):
        target = jnp.where(tslot[...] == j, codes[j], target)
    offset = toff[...].astype(F32)

    slot = lax.broadcasted_iota(jnp.int32, (CAP, TOK), 0)
    left, right, across = (lax.rem(x + s, NX) for s in (3, 1, 2))
    for i in range(2):
        for w in range(4):
            column = (x, (left, right)[i], (left, right)[i], across)[w]
            odd = (i, i, 1 - i, i)[w]
            which = (z * 8 + column * 2 + odd) * CAP
            rcode[i, pl.ds(w * CAP, CAP), :] = (slot + which).astype(F32)

    def hits(info, i, step):
        rows = rcode[i]
        if step is not None:
            rows = rows + ((lax.rem(z + step + NZ, NZ) - z) * 128).astype(F32)
        hit = rows == info[0:1, :]
        for j in range(1, A):
            hit = hit | (rows == info[j : j + 1, :])
        return hit

    def choose(hit):
        return jnp.where(hit, 1.0, 0.0).astype(BF16)

    named = jnp.concatenate(codes, axis=0)
    own_slab.wait()
    picks = []
    for d in range(2):
        step = 1 - 2 * d

        def marked(hit):
            return jnp.max(jnp.where(hit, 1.0, 0.0), axis=0, keepdims=True)

        last = marked(hits(named, d, 8))
        near = jnp.maximum(
            marked(hits(named, 0, 7 * step)), marked(hits(named, 1, 7 * step))
        )
        near = near * (1.0 - last)
        rest = 1.0 - last - near
        classes = jnp.concatenate([last, near, rest, jnp.zeros((13, TOK), F32)], axis=0)
        rank = jnp.dot(classes.astype(BF16), upper, preferred_element_type=F32)
        n_last = jnp.sum(last, axis=1, keepdims=True)
        n_near = jnp.sum(near, axis=1, keepdims=True)
        position = (
            last * rank[0:1]
            + near * (n_last + rank[1:2])
            + rest * (n_last + n_near + rank[2:3])
        )
        pick = jnp.where(tokens.astype(F32) == position, 1.0, 0.0)
        picks.append(pick)
        for c in range(2):
            rows = slice(c * 128, (c + 1) * 128)
            XS[d, rows] = jnp.dot(
                pick[rows].astype(BF16), X[0, 0], preferred_element_type=F32
            ).astype(BF16)
    for d in range(2):
        X[d, 7, 192:256] = jnp.zeros((64, SLAB), BF16)
        Z[d, 64:128] = jnp.zeros((64, SLAB), BF16)

    pl.semaphore_wait(barrier, 11)

    sides = (at_z(1), at_z(-1))

    def slab(k, d, c):
        begin, size = ((0, 64), (64, 64), (128, 64))[c] if k == 7 else (c * 128, 128)
        if k == 8:
            begin, size = 0, 64
        rows = pl.ds(begin, size)
        src = XS.at[d, rows] if k == 1 else X.at[d, k - 1, rows]
        dst = Z.at[d, rows] if k == 8 else X.at[d, k, rows]
        return push(src, dst, xs.at[d, k, c], xr.at[d, k, c], seg, sides[d])

    def meta(k, d):
        src = MS.at[d] if k == 1 else M.at[d, k - 1]
        return push(src, M.at[d, k], ms.at[d, k], mr.at[d, k], seg, sides[d])

    for c in range(2):
        for d in range(2):
            slab(1, d, c).start()

    first, second = head.at[pl.ds(0, BLOCK)], head.at[pl.ds(BLOCK, BLOCK)]

    def block(w, i):
        src = ((first, second), (second, first), (H.at[1, 0], H.at[1, 1]))[w - 1][i]
        return push(src, H.at[w, i], hs.at[w, i], hr.at[w, i], seg, at_x(1 - 2 * i))

    for i in range(2):
        block(1, i).start()

    squares = jnp.zeros((TOK, 128), F32)
    for c in range(SLAB // 128):
        part = X[0, 0, :, pl.ds(c * 128, 128)].astype(F32)
        squares = squares + part * part
    Sx[0] = jnp.sum(squares.T.reshape(16, 8, TOK), axis=0)

    def square(rel):
        return push(
            Sx.at[0], Sx.at[rel], ss.at[rel], sr.at[rel], lax.rem(seg + rel, 8), v
        )

    for rel in range(1, 8):
        square(rel).start()
    total = Sx[0]
    for rel in range(1, 8):
        square(rel).wait_recv()
        total = total + Sx[rel]
    scale = lax.rsqrt(jnp.sum(total, axis=0, keepdims=True) * (1.0 / D) + 1e-05)
    info = jnp.concatenate(codes + [scale, target, offset, offset], axis=0)
    M[0, 0] = info
    for d in range(2):
        MS[d] = lax.dot_general(
            info,
            picks[d],
            (((1,), (1,)), ((), ())),
            precision=lax.Precision.HIGHEST,
            preferred_element_type=F32,
        )
        meta(1, d).start()

    def keep(k, d, i, info, hit, picked):
        size = jnp.sum(jnp.where(hit, info[4:5, :], 0.0), axis=1, keepdims=True)
        normed = (picked * size * gain[...]).astype(BF16)
        for w in range(4):
            G[w, i, k, d] = normed[w * CAP : (w + 1) * CAP]

    def gather(k, d):
        info = M[d, k]
        for i in range(2):
            hit = hits(info, i, None)
            picked = jnp.dot(choose(hit), X[d, k], preferred_element_type=F32)
            keep(k, d, i, info, hit, picked)

    def gather_last():
        for i in range(2):
            info = M[i, 8]
            hit = hits(info, i, None)
            picked = jnp.dot(choose(hit)[:, 0:128], Z[i], preferred_element_type=F32)
            keep(0, 1, i, info, hit, picked)

    def spread(w, i, k0, count, logits):
        for d in range(2):
            for h in range(2):
                Pp[4 * i + 2 * h + d, pl.ds(k0, count), w] = logits[
                    :, d, :, 256 * h : 256 * (h + 1)
                ]

    def multiply(rows, w, i):
        return lax.dot_general(
            rows, H[w, i], (((1,), (1,)), ((), ())), preferred_element_type=F32
        )

    def products(w0, w1, k0, k1):
        count = k1 - k0

        def one(n, carry):
            w, i = n // 2, lax.rem(n, 2)
            rows = G[w, i, pl.ds(k0, count)].reshape(count * 2 * CAP, SLAB)
            logits = multiply(rows, w, i).reshape(count, 2, CAP, BLOCK).astype(BF16)
            spread(w, i, k0, count, logits)
            return carry

        lax.fori_loop(2 * w0, 2 * w1, one, 0)

    def products_flat(w0, w1, k):
        for w in range(w0, w1):
            for i in range(2):
                logits = multiply(G[w, i, k].reshape(2 * CAP, SLAB), w, i)
                spread(w, i, k, 1, logits.reshape(1, 2, CAP, BLOCK).astype(BF16))

    def products_last(w0, w1):
        for w in range(w0, w1):
            for i in range(2):
                logits = multiply(G[w, i, 0, 1], w, i).astype(BF16)
                for h in range(2):
                    Pp[4 * i + 2 * h + 1, 0, w] = logits[:, 256 * h : 256 * (h + 1)]

    def products_pair():
        for i in range(2):
            rows = G[3, i, pl.ds(0, 7)].reshape(7 * 2 * CAP, SLAB)
            logits = multiply(rows, 3, i).reshape(7, 2, CAP, BLOCK)
            mine = jnp.where(my_d == 0, logits[1:7, 0], logits[1:7, 1])
            others = jnp.where(my_d == 0, logits[1:7, 1], logits[1:7, 0])
            for h in range(2):
                span = slice(256 * h, 256 * (h + 1))
                Lm[2 * i + h] = mine[:, :, span]
                Ls[2 * i + h] = others[:, :, span]
                Pp[4 * i + 2 * h, 0, 3] = logits[0, 0, :, span].astype(BF16)

    def pair():
        return push(Ls, Lr, own.at[3], own.at[4], seg + 1 - 2 * my_d, v)

    def add_pair():
        for n in range(4):
            Pp[2 * n + my_d, 1:7, 3] = (Lm[n] + Lr[n]).astype(BF16)

    def partial(r, rel):
        w0, w1, k0, k1, _ = ROUNDS[r]
        dest = lax.rem(seg + rel, 8)
        part = (pl.ds(k0, k1 - k0), pl.ds(w0, w1 - w0))
        return push(
            Pp.at[(dest, *part)],
            Pr.at[(rel, *part)],
            ps.at[r, rel],
            pr.at[r, rel],
            dest,
            v,
        )

    def each_peer(r, act):
        side = ROUNDS[r][4]

        if r == PAIRED:
            for rel in (2, 4, 6):
                act(partial(r, rel))
            return

        def one(rel, carry):
            if side is None:
                act(partial(r, rel))
            else:

                @pl.when(lax.rem(seg + rel, 2) == side)
                def _():
                    act(partial(r, rel))

            return carry

        lax.fori_loop(1, 8, one, 0)

    def send(rounds):
        for r in rounds:
            each_peer(r, lambda copy: copy.start())

    def sent(rounds):
        for r in rounds:
            each_peer(r, lambda copy: copy.wait_send())

    def stats(rounds):
        for r in rounds:
            side = ROUNDS[r][4]
            if side is None:
                stats_of(r)
            else:
                pl.when(my_d == side)(functools.partial(stats_of, r))

    def stats_of(r):
        w0, w1, k0, k1, _ = ROUNDS[r]
        n = (w1 - w0) * CAP

        def arrive(rel, carry):
            partial(r, rel).wait_recv()
            return carry

        if r == PAIRED:
            for rel in (2, 4, 6):
                partial(r, rel).wait_recv()
        else:
            lax.fori_loop(1, 8, arrive, 0)

        last = r >= len(ROUNDS) - len(ROUND_E)

        def one(k, carry):
            span = pl.ds(w0, w1 - w0)
            logits = Pp[seg, k, span].reshape(n, 256).astype(F32)
            for rel in (2, 4, 6) if r == PAIRED else range(1, 8):
                logits = logits + Pr[rel, k, span].reshape(n, 256).astype(F32)
            info = M[my_i if last else my_d, 8 if last else k]
            rows = rcode[my_i, pl.ds(w0 * CAP, n), :]
            wanted = jnp.sum(
                jnp.where(rows == info[5:6, :], info[6:7, :] + 1.0, 0.0),
                axis=1,
                keepdims=True,
            )
            column = lax.broadcasted_iota(jnp.int32, (n, 256), 1) + 256 * my_h + 1
            peak = jnp.max(logits, axis=1, keepdims=True)
            mass = jnp.sum(jnp.exp(logits - peak), axis=1, keepdims=True)
            goal = jnp.sum(
                jnp.where(column.astype(F32) == wanted, logits, 0.0),
                axis=1,
                keepdims=True,
            )
            lane = lax.broadcasted_iota(jnp.int32, (n, 128), 1)
            St[k, pl.ds(w0 * CAP, n), :] = jnp.where(
                lane == 0, peak, jnp.where(lane == 1, mass, goal)
            )
            return carry

        if k1 - k0 == 1:
            one(k0, 0)
        else:
            lax.fori_loop(k0, k1, one, 0)

    def report(k):
        step = jnp.where(my_d == 0, -k, k)
        return push(Rs.at[k], Rr.at[k], ts.at[k], tr.at[k], seg, at_z(step))

    def turn(k):
        rows = St[k]
        Rs[k] = jnp.concatenate([rows, rows], axis=0).T[0:8]

    acc[...] = jnp.zeros((16, TOK), F32)

    def collect(k, step):
        plane = lax.rem(z + step + NZ, NZ) - z
        rows = rcode[my_i] + (plane * 128).astype(F32)
        columns = jnp.concatenate([Rr[k]] * 16, axis=0).T
        for j in range(A):
            match = rows == M[0, 0, j : j + 1, :]
            for q in range(3):
                acc[pl.ds(4 * q + j, 1), :] += jnp.sum(
                    jnp.where(match, columns[0:64, q : q + 1], 0.0), axis=0, keepdims=True
                )

    gather(0, 0)
    for w in range(4):
        for i in range(2):
            G[w, i, 0, 1] = jnp.zeros((CAP, SLAB), BF16)
    for c in own_head:
        c.wait()

    for n in range(3):
        shift = ((lax.rem(z + (7, 9, 8)[n], NZ) - z) * 128).astype(F32)
        for i in range(2):
            rows = rcode[i] + shift
            for j in range(A):
                table[n, i, :, pl.ds(j * TOK, TOK)] = jnp.where(
                    rows == named[j : j + 1], 1.0, 0.0
                )

    for k in range(1, 6):
        for d in range(2):
            slab(k, d, 0).wait_recv()
            slab(k + 1, d, 0).start()
        for d in range(2):
            slab(k, d, 1).wait_recv()
            meta(k, d).wait_recv()
            meta(k + 1, d).start()
            slab(k + 1, d, 1).start()
        for d in range(2):
            gather(k, d)
        if k == 1:
            for i in range(2):
                block(2, i).start()
        if k == 3:
            for i in range(2):
                block(1, i).wait()
                block(3, i).start()
            products(0, 2, 0, 4)
            send((0, 1))
        if k == 5:
            products(0, 2, 4, 6)
            send((2,))
            for i in range(2):
                block(2, i).wait()
            products(2, 3, 0, 6)
            send((3, 4))
            stats((0, 1))

    for d in range(2):
        slab(6, d, 0).wait_recv()
        slab(7, d, 0).start()
        slab(7, d, 1).start()
    for d in range(2):
        slab(6, d, 1).wait_recv()
        meta(6, d).wait_recv()
        meta(7, d).start()
        slab(7, d, 2).start()
    for d in range(2):
        gather(6, d)
    products(0, 3, 6, 7)
    send((5,))
    for d in range(2):
        slab(7, d, 0).wait_recv()
        meta(7, d).wait_recv()
        meta(8, d).start()
        slab(8, d, 0).start()
    for i in range(2):
        block(3, i).wait()
    products_pair()
    pair().start()
    send((7,))
    stats((2, 3, 4))
    pair().wait()
    add_pair()
    send((PAIRED,))

    for d in range(2):
        slab(7, d, 1).wait_recv()
        slab(7, d, 2).wait_recv()
    for d in range(2):
        gather(7, d)
    products_flat(0, 2, 7)
    send((8,))
    products_flat(2, 4, 7)
    send((9,))

    stats((5, 6, 7))
    for k in range(1, 7):
        turn(k)
        report(k).start()

    for d in range(2):
        slab(8, d, 0).wait_recv()
        meta(8, d).wait_recv()
    gather_last()
    products_last(0, 2)
    send((10,))
    products_last(2, 4)
    send((11,))


    @pl.when(my_d == 0)
    def _():
        turn(0)
        Rr[0] = Rs[0]

    def finish(n, rel):
        step = 8 if n == 2 else jnp.where(my_d == 0, -7, 7)
        place = n if n == 2 else my_d
        quarter = 2 * my_i + my_h
        return push(
            Qs.at[n // 2],
            Qr.at[place, quarter],
            qs.at[n // 2, rel],
            qr.at[place, quarter],
            lax.rem(seg + rel, 8),
            at_z(step),
        )

    def give(n, k):
        rows = St[k]
        turned = jnp.concatenate([rows, rows], axis=0).T
        lane = lax.broadcasted_iota(jnp.int32, (1, 128), 1)
        Qs[n // 2] = jnp.concatenate(
            [jnp.where(lane < 64, turned[0:1], turned[1:2]), turned[2:3]], axis=0
        )
        for rel in range(8):
            finish(n, rel).start()

    stats((8, 9))
    give(0, 7)
    stats((10, 11))

    @pl.when(my_d == 1)
    def _():
        give(2, 0)

    for k in range(1, 9):
        for d in range(2):
            for c in range(2 if k < 7 else (3, 1)[k - 7]):
                slab(k, d, c).wait_send()
            meta(k, d).wait_send()
    for rel in range(1, 8):
        square(rel).wait_send()
    sent(range(len(ROUNDS)))

    for k in range(1, 7):
        report(k).wait_recv()
        collect(k, jnp.where(my_d == 0, k, -k))

    @pl.when(my_d == 0)
    def _():
        collect(0, 0)

    peak, mass, goal = (acc[4 * q : 4 * q + 4] for q in range(3))
    have = mass > 0.5
    largest = jnp.max(jnp.where(have, peak, -1e30), axis=0, keepdims=True)
    weight = jnp.where(have, jnp.exp(jnp.where(have, peak - largest, 0.0)), 0.0)
    E[0] = jnp.concatenate(
        [
            largest,
            jnp.sum(mass * weight, axis=0, keepdims=True),
            jnp.sum(goal, axis=0, keepdims=True),
            jnp.zeros((5, TOK), F32),
        ],
        axis=0,
    )

    def share(rel):
        return push(E.at[0], E.at[rel], es.at[rel], er.at[rel], lax.rem(seg + rel, 8), v)

    for rel in range(1, 8):
        share(rel).start()
    for k in range(1, 7):
        report(k).wait_send()

    for rel in range(1, 8):
        share(rel).wait_recv()
    mine = []
    for n in range(3):
        for quarter in range(4):
            push(
                Qs.at[0], Qr.at[n, quarter], qs.at[0, 0], qr.at[n, quarter], seg, at_z(8)
            ).wait_recv()
        got = jnp.concatenate([Qr[n, quarter] for quarter in range(4)], axis=0)
        got = jnp.concatenate([got[:, 0:64], got[:, 64:128]], axis=0)
        for i in range(2):
            found = jnp.dot(
                got,
                table[n, i],
                precision=lax.Precision.HIGHEST,
                preferred_element_type=F32,
            )
            for h in range(2):
                row = 4 * i + 2 * h
                mine.append(
                    (found[row : row + 1], found[row + 8 : row + 9], found[row + 1 : row + 2])
                )
    peak, mass, goal = (jnp.concatenate(rows, axis=0) for rows in zip(*mine))
    here = mass > 0.5
    marked_peak = jnp.where(here, peak, -1e30)
    best = jnp.max(marked_peak, axis=0, keepdims=True)
    top_here = functools.reduce(
        jnp.maximum, [best[:, j * TOK : (j + 1) * TOK] for j in range(A)]
    )
    top = E[0, 0:1]
    for rel in range(1, 8):
        top = jnp.maximum(top, E[rel, 0:1])
    top = jnp.maximum(top, top_here)
    weight = jnp.exp(marked_peak - jnp.concatenate([top] * A, axis=1))
    mass_here = jnp.sum(jnp.where(here, mass * weight, 0.0), axis=0, keepdims=True)
    goal_here = jnp.sum(goal, axis=0, keepdims=True)
    mass = sum(mass_here[:, j * TOK : (j + 1) * TOK] for j in range(A))
    goal = sum(goal_here[:, j * TOK : (j + 1) * TOK] for j in range(A))
    for rel in range(8):
        mass = mass + E[rel, 1:2] * jnp.exp(E[rel, 0:1] - top)
        goal = goal + E[rel, 2:3]
    out[...] = goal - (top + jnp.log(mass))
    for rel in range(1, 8):
        share(rel).wait_send()

    for rel in range(8):
        finish(0, rel).wait_send()

    @pl.when(my_d == 1)
    def _():
        for rel in range(8):
            finish(2, rel).wait_send()


def per_device(hidden, norm_gain, head, allowed, target_slot, target_offset):
    vmem = pl.BlockSpec(memory_space=pltpu.VMEM)
    hbm = pl.BlockSpec(memory_space=pl.ANY)
    dma = pltpu.SemaphoreType.DMA
    out = pl.pallas_call(
        kernel,
        out_shape=jax.ShapeDtypeStruct((1, TOK), F32),
        in_specs=[hbm, vmem, hbm, vmem, vmem, vmem],
        out_specs=vmem,
        scratch_shapes=[
            pltpu.VMEM((2, 8, TOK, SLAB), BF16),
            pltpu.VMEM((2, TOK, SLAB), BF16),
            pltpu.VMEM((2, 128, SLAB), BF16),
            pltpu.VMEM((2, 9, 8, TOK), F32),
            pltpu.VMEM((2, 8, TOK), F32),
            pltpu.VMEM((4, 2, BLOCK, SLAB), BF16),
            pltpu.VMEM((4, 2, 8, 2, CAP, SLAB), BF16),
            pltpu.VMEM((8, 8, 4, CAP, 256), BF16),
            pltpu.VMEM((8, 8, 4, CAP, 256), BF16),
            pltpu.VMEM((8, 64, 128), F32),
            pltpu.VMEM((8, 8, 128), F32),
            pltpu.VMEM((8, 8, 128), F32),
            pltpu.VMEM((2, 2, 128), F32),
            pltpu.VMEM((3, 4, 2, 128), F32),
            pltpu.VMEM((3, 2, 64, A * TOK), F32),
            pltpu.VMEM((4, 6, CAP, 256), F32),
            pltpu.VMEM((4, 6, CAP, 256), F32),
            pltpu.VMEM((4, 6, CAP, 256), F32),
            pltpu.VMEM((2, 64, TOK), F32),
            pltpu.VMEM((8, 8, TOK), F32),
            pltpu.VMEM((8, 8, TOK), F32),
            pltpu.VMEM((16, TOK), F32),
            dma((2, 9, 3)),
            dma((2, 9, 3)),
            dma((2, 9)),
            dma((2, 9)),
            dma((4, 2)),
            dma((4, 2)),
            dma((len(ROUNDS), 8)),
            dma((len(ROUNDS), 8)),
            dma((8,)),
            dma((8,)),
            dma((8,)),
            dma((8,)),
            dma((8,)),
            dma((8,)),
            dma((2, 8)),
            dma((3, 4)),
            dma((5,)),
        ],
        compiler_params=pltpu.CompilerParams(
            collective_id=0, has_side_effects=True, vmem_limit_bytes=56 * 2**20
        ),
    )(
        hidden,
        norm_gain.reshape(1, SLAB),
        head,
        allowed,
        target_slot.reshape(1, TOK),
        target_offset.reshape(1, TOK),
    )
    return out.reshape(TOK)


def solution(mesh):
    return jax.shard_map(
        per_device,
        mesh=mesh,
        in_specs=(
            P("vocab", "segment"),
            P("segment"),
            P("vocab", "segment"),
            P(None, "vocab"),
            P("vocab"),
            P("vocab"),
        ),
        out_specs=P("vocab"),
        check_vma=False,
    )
```
